128 devices in a mesh: dp: 16 (over y, z), et: 8 (over x, core).
Axes of the slice: x: 4, y: 4, z: 4, core: 2. Of those that a mesh axis runs over, the one named last changes fastest.
Arguments:
- tokens: bfloat16 [2048, 4096], P('dp', 'et'), may hold values from -6 to 6
- routes: int32 [2048, 2], P('dp'), may hold values from 0 to 7, all different within a row; in each aligned block of 128 rows (0 to 127, 128 to 255, ...) at most 40 rows name the same one
- route_probs: float32 [2048, 2], P('dp'), may hold values from 0.2 to 1
- grad_out: bfloat16 [2048, 4096], P('dp', 'et'), may hold values from -6 to 6
- w_gate: bfloat16 [57344, 4096], P(('dp', 'et')), may hold values from -0.09375 to 0.09375
- w_up: bfloat16 [57344, 4096], P(('dp', 'et')), may hold values from -0.09375 to 0.09375
- w_down: bfloat16 [57344, 4096], P(('dp', 'et')), may hold values from -0.046875 to 0.046875
Outputs:
- layer_out: bfloat16 [2048, 4096], P('dp', 'et')
- grad_tokens: bfloat16 [2048, 4096], P('dp', 'et')
- grad_gate: bfloat16 [57344, 4096], P(('dp', 'et'))
- grad_up: bfloat16 [57344, 4096], P(('dp', 'et'))
- grad_down: bfloat16 [57344, 4096], P(('dp', 'et'))
The draws below stay inside these ranges and needn't reach their ends.
Inputs may be any that keep to these rules, and one draw needn't show every extreme that they name: `routes`: each row names 2 different experts of 8; within each aligned block of 128 rows (the tokens of one index of dp) no expert is named by more than 40 rows.
All inputs are finite; a program needn't handle non-finite values.
Results may differ from the reference program's by a relative error of at most 0.0058.
Values may be sent and summed in bfloat16 or wider, within the bound.
A program may use at most 192 MiB of HBM per device.

```python
import math
import jax
import jax.numpy as jnp
import numpy as np
from jax import lax

D = 4096
FF = 14336
EXPERTS_ALL = 8
TOP = 2
EXP = 4
TOK_DEV = 128
TOKENS = 2048
CAP = 40
N_DP = 16


def levels(key, extent, cuts, smallest, top_value):
    level, own = 1.0, jax.random.fold_in(key, 6)
    for position, parts in cuts:
        draws = jnp.exp(jax.random.uniform(jax.random.fold_in(own, position), (parts,), jnp.float32, smallest / len(cuts), top_value / len(cuts)))
        level = level * jnp.repeat(draws, extent[position] // parts).reshape([-1 if axis == position else 1 for axis in range(len(extent))])
    return level


def deal_out(stream_key, own, number, rows, number_of, top, most, skew):
    ranking = jax.random.permutation(stream_key, number_of)
    packed, common = portions_of(number_of, rows * top, most, skew, True), portions_of(number_of, rows * top, most, skew, False)
    places = jnp.arange(number_of)

    def named(tallies, turn):
        used = int((tallies > 0).sum())
        fixed = max(1, used // 4)
        moved = fixed + (places - fixed + turn * (used - fixed)) % max(1, number_of - fixed)
        return jnp.zeros((number_of,), jnp.int32).at[ranking[jnp.where(places < fixed, places, moved)]].set(jnp.asarray(tallies, jnp.int32))

    tallies = jnp.where(number % 4 == 0, named(packed, number // 4), named(common, number - number // 4 - 1))
    mixed = jax.random.permutation(jax.random.fold_in(own, 3), number_of)
    source_of, receiver = mixed[0:number_of // 2 * 2:2], mixed[1:number_of // 2 * 2:2]
    margin = jnp.minimum(tallies[source_of] - 1, most - tallies[receiver]) // 2
    margin = jnp.where((source_of == ranking[0]) | (receiver == ranking[0]) | (tallies[receiver] == 0), 0, jnp.maximum(margin, 0))
    moved = jax.random.randint(jax.random.fold_in(own, 4), (number_of // 2,), 0, 1 << 20) % (margin + 1)
    tallies = tallies.at[source_of].add(-moved).at[receiver].add(moved)
    items = jnp.searchsorted(jnp.cumsum(tallies), jnp.arange(rows * top), side="right").astype(jnp.int32)
    table = items.reshape(top, rows).T
    table = table[jax.random.permutation(jax.random.fold_in(own, 1), rows)]
    turn = jax.random.randint(jax.random.fold_in(own, 2), (rows, 1), 0, top)
    return jnp.take_along_axis(table, (jnp.arange(top)[None, :] + turn) % top, axis=1)


def portions_of(number_of, total, most, slope, full):
    weights = [(1 << 20) // math.isqrt(standing ** slope) + 1 for standing in range(1, number_of + 1)]
    largest = most if full else min(most, max(-(-total // number_of), total * weights[0] // sum(weights)))
    least = 1 if total - largest >= number_of - 1 else 0
    counts, surplus = [largest] + [least] * (number_of - 1), total - largest - least * (number_of - 1)
    while surplus > 0:
        candidates = [i for i in range(1, number_of) if counts[i] < largest] or [i for i in range(1, number_of) if counts[i] < most]
        mass, left = sum([weights[i] for i in candidates]), surplus
        for i in candidates:
            addition = min(most - counts[i], max(1, left * weights[i] // mass), surplus)
            counts[i] = counts[i] + addition
            surplus = surplus - addition
    return np.array(counts)


def normal_values(key, extent, width, bound, split=(), kind=jnp.bfloat16):
    gain = levels(key, extent, split, -0.22, 0.18) if split else 1.0
    array = jax.random.normal(key, extent, jnp.float32) * width * gain
    return jnp.minimum(jnp.maximum(array, -bound), bound).astype(kind)


def setup_inputs(seed: int = 0) -> dict:
    arg_keys = jax.random.split(jax.random.key(seed), 8)
    tokens = normal_values(arg_keys[0], (TOKENS, D), 1.0, 6.0, ((0, 16), (1, 8)))
    routes_keys = jax.random.split(jax.random.fold_in(arg_keys[1], 1), TOKENS // TOK_DEV)
    routes_turns = jax.random.permutation(jax.random.fold_in(arg_keys[1], 3), TOKENS // TOK_DEV)
    routes = jax.vmap(lambda own, number: deal_out(jax.random.fold_in(arg_keys[1], 2), own, number, TOK_DEV, EXPERTS_ALL, TOP, CAP, 2))(routes_keys, routes_turns).reshape((TOKENS, TOP))
    route_probs = jnp.clip(0.2 + 0.8 * jax.random.uniform(arg_keys[2], (TOKENS, TOP), jnp.float32) ** levels(arg_keys[2], (TOKENS, TOP), ((0, 16),), -0.2, 0.2), 0.2, 1.0)
    grad_out = normal_values(arg_keys[3], (TOKENS, D), 1.0, 6.0, ((0, 16), (1, 8)))
    w_gate = normal_values(arg_keys[4], (EXP * FF, D), D ** -0.5, 0.09375, ((0, 128),))
    w_up = normal_values(arg_keys[5], (EXP * FF, D), D ** -0.5, 0.09375, ((0, 128),))
    w_down = normal_values(arg_keys[6], (EXP * FF, D), FF ** -0.5, 0.046875, ((0, 128),))
    return {"tokens": tokens, "routes": routes, "route_probs": route_probs, "grad_out": grad_out, "w_gate": w_gate, "w_up": w_up, "w_down": w_down}


def reference(tokens, routes, route_probs, grad_out, w_gate, w_up, w_down):
    token_count = tokens.shape[0]
    features = tokens.shape[1]
    most_rows = N_DP * CAP
    positions = jnp.arange(most_rows, dtype=jnp.int32)
    layer_acc = jnp.zeros((token_count, features), jnp.float32)
    token_acc = jnp.zeros((token_count, features), jnp.float32)
    gate_parts = []
    up_parts = []
    down_parts = []
    contract_last = (((1,), (1,)), ((), ()))
    contract_first = (((0,), (0,)), ((), ()))
    for expert in range(EXP):
        matches = routes == expert
        member = jnp.any(matches, axis=1)
        live_count = jnp.sum(member.astype(jnp.int32))
        chosen = jnp.nonzero(member, size=most_rows, fill_value=0)[0].astype(jnp.int32)
        valid_rows = positions < live_count
        weight_all = jnp.sum(jnp.where(matches, route_probs, jnp.zeros((), route_probs.dtype)), axis=1)
        weight = jnp.where(valid_rows, weight_all[chosen], jnp.zeros((), weight_all.dtype))
        rows_x = jnp.where(valid_rows[:, None], tokens[chosen], jnp.zeros((), tokens.dtype))
        scaled = (weight[:, None] * grad_out[chosen].astype(jnp.float32)).astype(jnp.bfloat16)
        first_row = expert * FF
        gate_w = w_gate[first_row:first_row + FF]
        up_w = w_up[first_row:first_row + FF]
        down_w = w_down[first_row:first_row + FF]
        gate_pre = lax.dot_general(rows_x, gate_w, contract_last, preferred_element_type=jnp.float32)
        up_pre = lax.dot_general(rows_x, up_w, contract_last, preferred_element_type=jnp.float32)
        squash = jax.nn.sigmoid(gate_pre)
        active = gate_pre * squash
        hidden = (active * up_pre).astype(jnp.bfloat16)
        expert_out = jnp.dot(hidden, down_w, preferred_element_type=jnp.float32)
        d_hidden = lax.dot_general(scaled, down_w, contract_last, preferred_element_type=jnp.float32)
        d_gate = (d_hidden * up_pre * squash * (1.0 + gate_pre * (1.0 - squash))).astype(jnp.bfloat16)
        d_up = (d_hidden * active).astype(jnp.bfloat16)
        d_rows = jnp.dot(d_gate, gate_w, preferred_element_type=jnp.float32) + jnp.dot(d_up, up_w, preferred_element_type=jnp.float32)
        layer_acc = layer_acc.at[chosen].add(weight[:, None] * expert_out)
        token_acc = token_acc.at[chosen].add(d_rows)
        gate_parts.append(lax.dot_general(d_gate, rows_x, contract_first, preferred_element_type=jnp.float32).astype(jnp.bfloat16))
        up_parts.append(lax.dot_general(d_up, rows_x, contract_first, preferred_element_type=jnp.float32).astype(jnp.bfloat16))
        down_parts.append(lax.dot_general(hidden, scaled, contract_first, preferred_element_type=jnp.float32).astype(jnp.bfloat16))
    return (layer_acc.astype(jnp.bfloat16), token_acc.astype(jnp.bfloat16), jnp.concatenate(gate_parts, axis=0), jnp.concatenate(up_parts, axis=0), jnp.concatenate(down_parts, axis=0))
```

```python
import functools

import jax
import jax.numpy as jnp
from jax import lax
from jax.experimental import pallas as pl
from jax.experimental.pallas import tpu as pltpu
from jax.sharding import PartitionSpec as P

MESH = pl.DeviceIdType.MESH
EXP = 4
CAP = 40
SIDE = 4
ROWS = SIDE * CAP
HALF = ROWS // 2
KCH = 8
F32 = jnp.float32
BF16 = jnp.bfloat16
NT = (((1,), (1,)), ((), ()))
VMEM_LIMIT = 58 * 1024 * 1024


def place():
    dp = lax.axis_index("dp")
    et = lax.axis_index("et")
    return lax.div(dp, SIDE), lax.rem(dp, SIDE), lax.div(et, 2), lax.rem(et, 2)


def turn(value, by):
    return lax.rem(value + by, SIDE)


def device(y, z, x, c):
    return (y * SIDE + z, x * 2 + c)


def remote(src, dst, send_sem, recv_sem, target):
    return pltpu.make_async_remote_copy(
        src_ref=src, dst_ref=dst, send_sem=send_sem, recv_sem=recv_sem, device_id=target, device_id_type=MESH
    )


def greet(y, z, x, c):
    barrier = pltpu.get_barrier_semaphore()
    others = [device(y, z, x, 1 - c)]
    others += [device(y, z, turn(x, 1), c), device(y, z, turn(x, 3), c)]
    others += [device(y, turn(z, 1), x, c), device(y, turn(z, 3), x, c)]
    others += [device(turn(y, by), z, x, c) for by in (1, 2, 3)]
    for other in others:
        pl.semaphore_signal(barrier, inc=1, device_id=other, device_id_type=MESH)
    pl.semaphore_wait(barrier, len(others))


def pack_rows(routes, probs, tok, cot, pack):
    count = tok.shape[0]
    route = routes[...].astype(F32)
    prob = probs[...]
    square = (count, count)
    r0 = jnp.transpose(jnp.broadcast_to(route[:, 0:1], square))[:CAP]
    r1 = jnp.transpose(jnp.broadcast_to(route[:, 1:2], square))[:CAP]
    p0 = jnp.transpose(jnp.broadcast_to(prob[:, 0:1], square))[:CAP]
    p1 = jnp.transpose(jnp.broadcast_to(prob[:, 1:2], square))[:CAP]
    first = lax.broadcasted_iota(jnp.int32, square, 0)
    second = lax.broadcasted_iota(jnp.int32, square, 1)
    before = jnp.where(first < second, 1.0, 0.0).astype(BF16)
    slot = lax.broadcasted_iota(jnp.int32, (CAP, count), 0).astype(F32)
    x_all = tok[...]
    d_all = cot[...]
    for e in range(EXP):
        in0 = jnp.where(r0 == e, 1.0, 0.0)
        in1 = jnp.where(r1 == e, 1.0, 0.0)
        member = in0 + in1
        placed = jnp.dot(member.astype(BF16), before, preferred_element_type=F32)
        pick = jnp.where(placed == slot, member, 0.0)
        weight = jnp.sum(pick * (in0 * p0 + in1 * p1), axis=1, keepdims=True)
        pick = pick.astype(BF16)
        chosen = jnp.dot(pick, x_all, preferred_element_type=F32)
        scaled = weight * jnp.dot(pick, d_all, preferred_element_type=F32)
        pack[e] = jnp.concatenate([chosen, scaled], axis=0).astype(BF16)


def gather_kernel(
    routes, probs, tok, cot, wg, wu, wd, xg, sg, h_out, dg_out, du_out,
    pack, recv, xb, sb, wgv, wuv, wdv, acc_g, acc_u, acc_d,
    w_sem, out_sem, ys, yr, n1s, n1r, h1s, h1r, n2s, n2r, h2s, h2r, ps, pr,
):
    y, z, x, c = place()
    loads = []
    for i, (src, dst) in enumerate(((wg, wgv), (wu, wuv), (wd, wdv))):
        for k in range(KCH):
            load = pltpu.make_async_copy(src.at[:, pl.ds(k * 512, 512)], dst.at[k], w_sem.at[i, k])
            load.start()
            loads.append(load)
    pack_rows(routes, probs, tok, cot, pack)
    greet(y, z, x, c)
    sends = []
    y_copies = []
    for by in (1, 2, 3):
        e = turn(y, by)
        copy = remote(pack.at[e], recv.at[y], ys.at[by - 1], yr.at[by - 1], device(e, z, x, c))
        copy.start()
        sends.append(copy)
    recv[y] = pack[y]
    for by in (1, 2, 3):
        source = turn(y, SIDE - by)
        remote(pack.at[source], recv.at[source], ys.at[by - 1], yr.at[by - 1], device(source, z, x, c)).wait_recv()
    parts = [recv[i].astype(F32) for i in range(SIDE)]
    own = x * 2 + c
    xb[z, own] = jnp.concatenate([part[:CAP] for part in parts], axis=0).astype(BF16)
    sb[z, own] = jnp.concatenate([part[CAP:] for part in parts], axis=0).astype(BF16)

    partner = device(y, z, x, 1 - c)
    low, high = pl.ds(0, HALF), pl.ds(HALF, HALF)
    off = (0, 3, 1, 2)
    bufs = (xb, sb)

    def chunk(a, first, second):
        if a == 0:
            return xb.at[second, first * 2 + c]
        return sb.at[first, second * 2 + c]

    def mine(a):
        return (x, z) if a == 0 else (z, x)

    def first_dev(a, place_on):
        return device(y, z, place_on, c) if a == 0 else device(y, place_on, x, c)

    def second_dev(a, place_on):
        return device(y, place_on, x, c) if a == 0 else device(y, z, place_on, c)

    def to_partner(a, i, j):
        f, s = mine(a)
        ref = chunk(a, turn(f, off[j]), turn(s, off[i]))
        copy = remote(ref, ref, ps.at[a, i, j], pr.at[a, i, j], partner)
        copy.start()
        sends.append(copy)

    def from_partner(a, i, j):
        f, s = mine(a)
        first, second = turn(f, off[j]), turn(s, off[i])
        if a == 0:
            ref = xb.at[second, first * 2 + (1 - c)]
        else:
            ref = sb.at[first, second * 2 + (1 - c)]
        remote(ref, ref, ps.at[a, i, j], pr.at[a, i, j], partner).wait_recv()

    def first_send(a):
        f, s = mine(a)
        ref = chunk(a, f, s)
        for d, by in ((0, 1), (1, 3)):
            copy = remote(ref, ref, n1s.at[a, d], n1r.at[a, d], first_dev(a, turn(f, by)))
            copy.start()
            sends.append(copy)

    def first_recv(a, d):
        f, s = mine(a)
        source = turn(f, 3 if d == 0 else 1)
        ref = chunk(a, source, s)
        remote(ref, ref, n1s.at[a, d], n1r.at[a, d], first_dev(a, source)).wait_recv()
        part = ref.at[low if d == 0 else high]
        copy = remote(part, part, h1s.at[a, d], h1r.at[a, d], first_dev(a, turn(f, 1 if d == 0 else 3)))
        copy.start()
        sends.append(copy)

    def first_far(a):
        f, s = mine(a)
        ref = chunk(a, turn(f, 2), s)
        for d, part in ((0, ref.at[low]), (1, ref.at[high])):
            remote(part, part, h1s.at[a, d], h1r.at[a, d], first_dev(a, turn(f, 3 if d == 0 else 1))).wait_recv()

    def second_send(a, j):
        f, s = mine(a)
        ref = chunk(a, turn(f, off[j]), s)
        for d, by in ((0, 1), (1, 3)):
            copy = remote(ref, ref, n2s.at[a, j, d], n2r.at[a, j, d], second_dev(a, turn(s, by)))
            copy.start()
            sends.append(copy)

    def second_recv(a, j, d):
        f, s = mine(a)
        source = turn(s, 3 if d == 0 else 1)
        ref = chunk(a, turn(f, off[j]), source)
        remote(ref, ref, n2s.at[a, j, d], n2r.at[a, j, d], second_dev(a, source)).wait_recv()
        part = ref.at[low if d == 0 else high]
        copy = remote(part, part, h2s.at[a, j, d], h2r.at[a, j, d], second_dev(a, turn(s, 1 if d == 0 else 3)))
        copy.start()
        sends.append(copy)

    def second_far(a, j):
        f, s = mine(a)
        ref = chunk(a, turn(f, off[j]), turn(s, 2))
        for d, part in ((0, ref.at[low]), (1, ref.at[high])):
            remote(part, part, h2s.at[a, j, d], h2r.at[a, j, d], second_dev(a, turn(s, 3 if d == 0 else 1))).wait_recv()

    for a in (0, 1):
        first_send(a)
    for a in (0, 1):
        second_send(a, 0)
        to_partner(a, 0, 0)
    for d in (0, 1):
        for a in (0, 1):
            first_recv(a, d)
            second_send(a, 1 + d)
            to_partner(a, 0, 1 + d)
    for a in (0, 1):
        first_far(a)
        second_send(a, 3)
        to_partner(a, 0, 3)
    for j in range(SIDE):
        for d in (0, 1):
            for a in (0, 1):
                second_recv(a, j, d)
                to_partner(a, 1 + d, j)
        if j > 0:
            for a in (0, 1):
                second_far(a, j - 1)
                to_partner(a, 3, j - 1)
    for a in (0, 1):
        second_far(a, SIDE - 1)
        to_partner(a, 3, SIDE - 1)
    for a in (0, 1):
        for i in range(SIDE):
            for j in range(SIDE):
                from_partner(a, i, j)
    out_x = pltpu.make_async_copy(xb, xg, out_sem.at[0])
    out_s = pltpu.make_async_copy(sb, sg, out_sem.at[1])
    out_x.start()
    out_s.start()
    for load in loads:
        load.wait()
    acc_g[...] = jnp.zeros_like(acc_g)
    acc_u[...] = jnp.zeros_like(acc_u)
    acc_d[...] = jnp.zeros_like(acc_d)

    def step(k, carry):
        rows_x = xb[:, k].reshape(SIDE * ROWS, 512)
        rows_s = sb[:, k].reshape(SIDE * ROWS, 512)
        acc_g[...] += lax.dot_general(rows_x, wgv[k], NT, preferred_element_type=F32)
        acc_u[...] += lax.dot_general(rows_x, wuv[k], NT, preferred_element_type=F32)
        acc_d[...] += lax.dot_general(rows_s, wdv[k], NT, preferred_element_type=F32)
        return carry

    lax.fori_loop(0, KCH, step, 0)

    def activate(i, carry):
        rows = pl.ds(pl.multiple_of(i * 32, 32), 32)
        gate = acc_g[rows, :]
        up = acc_u[rows, :]
        d_hidden = acc_d[rows, :]
        squash = jax.nn.sigmoid(gate)
        active = gate * squash
        h_out[rows, :] = (active * up).astype(BF16)
        dg_out[rows, :] = (d_hidden * up * squash * (1.0 + gate * (1.0 - squash))).astype(BF16)
        du_out[rows, :] = (d_hidden * active).astype(BF16)
        return carry

    lax.fori_loop(0, SIDE * ROWS // 32, activate, 0)
    out_x.wait()
    out_s.wait()
    for copy in sends:
        copy.wait_send()


def grads_kernel(xg, sg, h, dg, du, gate_out, up_out, down_out, ht, dgt, dut):
    @pl.when(pl.program_id(0) == 0)
    def _():
        ht[...] = jnp.transpose(h[...])
        dgt[...] = jnp.transpose(dg[...])
        dut[...] = jnp.transpose(du[...])

    rows_x = xg[...].reshape(SIDE * ROWS, 512)
    rows_s = sg[...].reshape(SIDE * ROWS, 512)
    gate_out[...] = jnp.dot(dgt[...], rows_x, preferred_element_type=F32).astype(BF16)
    up_out[...] = jnp.dot(dut[...], rows_x, preferred_element_type=F32).astype(BF16)
    down_out[...] = jnp.dot(ht[...], rows_s, preferred_element_type=F32).astype(BF16)


def scatter_kernel(
    routes, probs, h, dg, du, wg, wu, wd, layer_out, token_out,
    wgv, wuv, wdv, own, psend, precv, far, farr, mid, midr, far2, far2r, mid2, mid2r, first_sum, ysend, yrecv,
    w_sem, ps, pr, fs, fr, ms, mr, f2s, f2r, m2s, m2r, ys, yr,
):
    y, z, x, c = place()
    for k in range(KCH):
        for i, (src, dst) in enumerate(((wg, wgv), (wu, wuv), (wd, wdv))):
            pltpu.make_async_copy(src.at[:, pl.ds(k * 512, 512)], dst.at[k], w_sem.at[i, k]).start()
    greet(y, z, x, c)
    partner = device(y, z, x, 1 - c)
    low, high = pl.ds(0, HALF), pl.ds(HALF, HALF)

    def offset(j):
        return lax.rem(2 + j + lax.div(j, 2) + 2 * lax.div(j, 3), SIDE)

    def first_dev(a, by):
        return device(y, turn(z, by), x, c) if a == 0 else device(y, z, turn(x, by), c)

    def second_dev(a, by):
        return device(y, z, turn(x, by), c) if a == 0 else device(y, turn(z, by), x, c)

    def partner_copy(a, j):
        return remote(psend.at[a, j], precv.at[a, j], ps.at[a, j], pr.at[a, j], partner)

    def compute(j):
        at = turn(x, offset(j))
        rows = h[...].reshape(SIDE * ROWS, 448)
        keep = jnp.dot(rows, wdv[at * 2 + c], preferred_element_type=F32)
        own[0, j] = keep.reshape(SIDE, ROWS, 512)
        give = jnp.dot(rows, wdv[at * 2 + 1 - c], preferred_element_type=F32)
        psend[0, j] = give.astype(BF16).reshape(SIDE, ROWS, 512)
        partner_copy(0, j).start()
        at = turn(z, offset(j))
        rows_g, rows_u = dg[at], du[at]

        def columns(i, carry):
            keep = jnp.dot(rows_g, wgv[i * 2 + c], preferred_element_type=F32)
            keep += jnp.dot(rows_u, wuv[i * 2 + c], preferred_element_type=F32)
            own[1, j, i] = keep
            give = jnp.dot(rows_g, wgv[i * 2 + 1 - c], preferred_element_type=F32)
            give += jnp.dot(rows_u, wuv[i * 2 + 1 - c], preferred_element_type=F32)
            psend[1, j, i] = give.astype(BF16)
            return carry

        lax.fori_loop(0, SIDE, columns, 0)
        partner_copy(1, j).start()

    def here(a):
        return z if a == 0 else x

    def pair_sum(a, j, by):
        at = turn(here(a), by)
        return own[a, j, at] + precv[a, j, at].astype(F32)

    def far_copy(a, j, d):
        part = high if d == 0 else low
        return remote(far.at[a, j, part], farr.at[a, j, d], fs.at[a, j, d], fr.at[a, j, d], first_dev(a, 1 if d == 0 else 3))

    def send_far(a, j):
        partner_copy(a, j).wait_recv()
        far[a, j] = pair_sum(a, j, 2).astype(BF16)
        far_copy(a, j, 0).start()
        far_copy(a, j, 1).start()

    def mid_copy(a, j, d):
        return remote(mid.at[a, j, d], midr.at[a, j, d], ms.at[a, j, d], mr.at[a, j, d], first_dev(a, 1 if d == 0 else 3))

    def send_mid(a, j):
        for d, by in ((0, 1), (1, 3)):
            total = pair_sum(a, j, by)
            far_copy(a, j, d).wait_recv()
            part = farr[a, j, d].astype(F32)
            if d == 0:
                total = jnp.concatenate([total[:HALF], total[HALF:] + part], axis=0)
            else:
                total = jnp.concatenate([total[:HALF] + part, total[HALF:]], axis=0)
            mid[a, j, d] = total.astype(BF16)
            mid_copy(a, j, d).start()

    def finish_first(a, j):
        total = pair_sum(a, j, 0)
        for d in (0, 1):
            mid_copy(a, j, d).wait_recv()
            total = total + midr[a, j, d].astype(F32)
        first_sum[a, j] = total

    def far2_copy(a, d):
        part = high if d == 0 else low
        return remote(far2.at[a, part], far2r.at[a, d], f2s.at[a, d], f2r.at[a, d], second_dev(a, 1 if d == 0 else 3))

    def mid2_copy(a, d):
        return remote(mid2.at[a, d], mid2r.at[a, d], m2s.at[a, d], m2r.at[a, d], second_dev(a, 1 if d == 0 else 3))

    def send_far2(a):
        far2[a] = first_sum[a, 0].astype(BF16)
        far2_copy(a, 0).start()
        far2_copy(a, 1).start()

    def send_mid2(a, d):
        total = first_sum[a, 2 if d == 0 else 1]
        far2_copy(a, d).wait_recv()
        part = far2r[a, d].astype(F32)
        if d == 0:
            total = jnp.concatenate([total[:HALF], total[HALF:] + part], axis=0)
        else:
            total = jnp.concatenate([total[:HALF] + part, total[HALF:]], axis=0)
        mid2[a, d] = total.astype(BF16)
        mid2_copy(a, d).start()

    def finish_second(a):
        total = first_sum[a, 3]
        for d in (0, 1):
            mid2_copy(a, d).wait_recv()
            total = total + mid2r[a, d].astype(F32)
        return total

    for i, (src, dst) in enumerate(((wg, wgv), (wu, wuv), (wd, wdv))):
        for k in range(KCH):
            pltpu.make_async_copy(src.at[:, pl.ds(k * 512, 512)], dst.at[k], w_sem.at[i, k]).wait()

    def pipeline(t, carry):
        @pl.when(t < SIDE)
        def _():
            compute(t)

        @pl.when((t >= 1) & (t <= SIDE))
        def _():
            send_far(0, t - 1)
            send_far(1, t - 1)

        @pl.when(t >= 2)
        def _():
            send_mid(0, t - 2)
            send_mid(1, t - 2)

        return carry

    lax.fori_loop(0, SIDE + 2, pipeline, 0)
    for a in (0, 1):
        finish_first(a, 0)
        send_far2(a)
    for a in (0, 1):
        finish_first(a, 1)
        send_mid2(a, 1)
    for a in (0, 1):
        finish_first(a, 2)
        send_mid2(a, 0)
    for a in (0, 1):
        finish_first(a, 3)
    totals = [finish_second(a) for a in (0, 1)]
    for i in range(SIDE):
        piece = [total[i * CAP:(i + 1) * CAP] for total in totals]
        ysend[i] = jnp.concatenate(piece, axis=0).astype(BF16)
    y_copies = []
    for by in (1, 2, 3):
        target = turn(y, by)
        copy = remote(ysend.at[target], yrecv.at[y], ys.at[by - 1], yr.at[by - 1], device(target, z, x, c))
        copy.start()
        y_copies.append(copy)
    yrecv[y] = ysend[y]

    count = layer_out.shape[0]
    route = routes[...]
    prob = probs[...]
    square = (count, count)
    first = lax.broadcasted_iota(jnp.int32, square, 0)
    second = lax.broadcasted_iota(jnp.int32, square, 1)
    before = jnp.where(second < first, 1.0, 0.0).astype(BF16)
    lane = lax.broadcasted_iota(jnp.int32, (count, 2 * CAP), 1).astype(F32)
    r0 = jnp.broadcast_to(route[:, 0:1], (count, 2 * CAP))
    r1 = jnp.broadcast_to(route[:, 1:2], (count, 2 * CAP))
    picks = []
    for e in range(EXP):
        member = jnp.where(r0 == e, 1.0, 0.0) + jnp.where(r1 == e, 1.0, 0.0)
        placed = jnp.dot(before, member.astype(BF16), preferred_element_type=F32)
        pick_out = jnp.where(placed == lane, member, 0.0).astype(BF16)
        pick_dx = jnp.where(placed + CAP == lane, member, 0.0).astype(BF16)
        pick_out = jnp.where(lane < CAP, pick_out.astype(F32), 0.0).astype(BF16)
        weight = jnp.where(route[:, 0:1] == e, prob[:, 0:1], 0.0) + jnp.where(route[:, 1:2] == e, prob[:, 1:2], 0.0)
        picks.append((pick_out, pick_dx, weight))
    for by in (1, 2, 3):
        source = turn(y, SIDE - by)
        remote(ysend.at[source], yrecv.at[source], ys.at[by - 1], yr.at[by - 1], device(source, z, x, c)).wait_recv()
    layer = jnp.zeros(layer_out.shape, F32)
    token = jnp.zeros(token_out.shape, F32)
    for e in range(EXP):
        pick_out, pick_dx, weight = picks[e]
        rows = yrecv[e]
        layer = layer + weight * jnp.dot(pick_out, rows, preferred_element_type=F32)
        token = token + jnp.dot(pick_dx, rows, preferred_element_type=F32)
    layer_out[...] = layer.astype(BF16)
    token_out[...] = token.astype(BF16)

    for copy in y_copies:
        copy.wait_send()
    for a in (0, 1):
        for d in (0, 1):
            far2_copy(a, d).wait_send()
            mid2_copy(a, d).wait_send()

    def drain(j, carry):
        for a in (0, 1):
            partner_copy(a, j).wait_send()
            for d in (0, 1):
                far_copy(a, j, d).wait_send()
                mid_copy(a, j, d).wait_send()
        return carry

    lax.fori_loop(0, SIDE, drain, 0)


def per_device(tokens, routes, route_probs, grad_out, w_gate, w_up, w_down):
    hidden_units, width = w_gate.shape
    rows = SIDE * ROWS
    vmem = pl.BlockSpec(memory_space=pltpu.VMEM)
    anywhere = pl.BlockSpec(memory_space=pl.ANY)
    dma = pltpu.SemaphoreType.DMA
    gathered = jax.ShapeDtypeStruct((SIDE, KCH, ROWS, 512), BF16)
    small = jax.ShapeDtypeStruct((rows, hidden_units), BF16)
    weight_buf = pltpu.VMEM((KCH, hidden_units, 512), BF16)
    xg, sg, h, dg, du = pl.pallas_call(
        gather_kernel,
        out_shape=(gathered, gathered, small, small, small),
        in_specs=[vmem] * 4 + [anywhere] * 3,
        out_specs=(anywhere, anywhere, vmem, vmem, vmem),
        scratch_shapes=[
            pltpu.VMEM((EXP, 2 * CAP, 512), BF16),
            pltpu.VMEM((SIDE, 2 * CAP, 512), BF16),
            pltpu.VMEM((SIDE, KCH, ROWS, 512), BF16),
            pltpu.VMEM((SIDE, KCH, ROWS, 512), BF16),
            weight_buf, weight_buf, weight_buf,
            pltpu.VMEM((rows, hidden_units), F32),
            pltpu.VMEM((rows, hidden_units), F32),
            pltpu.VMEM((rows, hidden_units), F32),
            dma((3, KCH)), dma((2,)), dma((3,)), dma((3,)),
            dma((2, 2)), dma((2, 2)), dma((2, 2)), dma((2, 2)),
            dma((2, 4, 2)), dma((2, 4, 2)), dma((2, 4, 2)), dma((2, 4, 2)),
            dma((2, 4, 4)), dma((2, 4, 4)),
        ],
        compiler_params=pltpu.CompilerParams(collective_id=0, has_side_effects=True, vmem_limit_bytes=VMEM_LIMIT),
        name="gather_rows",
    )(routes, route_probs, tokens, grad_out, w_gate, w_up, w_down)

    block = pl.BlockSpec((SIDE, 1, ROWS, 512), lambda k: (0, k, 0, 0))
    whole = pl.BlockSpec((rows, hidden_units), lambda k: (0, 0))
    grad_spec = pl.BlockSpec((hidden_units, 512), lambda k: (0, k))
    grad_shape = jax.ShapeDtypeStruct((hidden_units, width), BF16)
    grad_gate, grad_up, grad_down = pl.pallas_call(
        grads_kernel,
        grid=(KCH,),
        out_shape=(grad_shape,) * 3,
        in_specs=[block, block, whole, whole, whole],
        out_specs=(grad_spec,) * 3,
        scratch_shapes=[pltpu.VMEM((hidden_units, rows), BF16)] * 3,
        compiler_params=pltpu.CompilerParams(vmem_limit_bytes=VMEM_LIMIT),
        name="weight_grads",
    )(xg, sg, h, dg, du)

    stacked = (SIDE, ROWS, hidden_units)
    token_shape = jax.ShapeDtypeStruct(tokens.shape, BF16)
    layer_out, grad_tokens = pl.pallas_call(
        scatter_kernel,
        out_shape=(token_shape, token_shape),
        in_specs=[vmem] * 5 + [anywhere] * 3,
        out_specs=(vmem, vmem),
        scratch_shapes=[
            weight_buf, weight_buf, weight_buf,
            pltpu.VMEM((2, SIDE, SIDE, ROWS, 512), F32),
            pltpu.VMEM((2, SIDE, SIDE, ROWS, 512), BF16),
            pltpu.VMEM((2, SIDE, SIDE, ROWS, 512), BF16),
            pltpu.VMEM((2, SIDE, ROWS, 512), BF16),
            pltpu.VMEM((2, SIDE, 2, HALF, 512), BF16),
            pltpu.VMEM((2, SIDE, 2, ROWS, 512), BF16),
            pltpu.VMEM((2, SIDE, 2, ROWS, 512), BF16),
            pltpu.VMEM((2, ROWS, 512), BF16),
            pltpu.VMEM((2, 2, HALF, 512), BF16),
            pltpu.VMEM((2, 2, ROWS, 512), BF16),
            pltpu.VMEM((2, 2, ROWS, 512), BF16),
            pltpu.VMEM((2, SIDE, ROWS, 512), F32),
            pltpu.VMEM((SIDE, 2 * CAP, 512), BF16),
            pltpu.VMEM((SIDE, 2 * CAP, 512), BF16),
            dma((3, KCH)), dma((2, 4)), dma((2, 4)),
            dma((2, 4, 2)), dma((2, 4, 2)), dma((2, 4, 2)), dma((2, 4, 2)),
            dma((2, 2)), dma((2, 2)), dma((2, 2)), dma((2, 2)),
            dma((3,)), dma((3,)),
        ],
        compiler_params=pltpu.CompilerParams(collective_id=1, has_side_effects=True, vmem_limit_bytes=VMEM_LIMIT),
        name="scatter_sums",
    )(routes, route_probs, h.reshape(stacked), dg.reshape(stacked), du.reshape(stacked), w_gate, w_up, w_down)
    return layer_out, grad_tokens, grad_gate, grad_up, grad_down


def solution(mesh):
    return jax.shard_map(
        per_device,
        mesh=mesh,
        in_specs=(
            P("dp", "et"),
            P("dp", None),
            P("dp", None),
            P("dp", "et"),
            P(("dp", "et"), None),
            P(("dp", "et"), None),
            P(("dp", "et"), None),
        ),
        out_specs=(
            P("dp", "et"),
            P("dp", "et"),
            P(("dp", "et"), None),
            P(("dp", "et"), None),
            P(("dp", "et"), None),
        ),
        check_vma=False,
    )
```

```python
import jax
import jax.numpy as jnp
from jax import lax
from jax.experimental import pallas as pl
from jax.experimental.pallas import tpu as pltpu
from jax.sharding import PartitionSpec as P

MESH = pl.DeviceIdType.MESH
EXP = 4
CAP = 40
SIDE = 4
ROWS = SIDE * CAP
ALL_ROWS = SIDE * ROWS
HALF = ROWS // 2
ETS = 8
WIDE = 512
PART = 256
F32 = jnp.float32
BF16 = jnp.bfloat16
NT = (((1,), (1,)), ((), ()))
FLOWS = (0, 1)
VMEM_LIMIT = 60 * 1024 * 1024


def place():
    dp = lax.axis_index("dp")
    et = lax.axis_index("et")
    return lax.div(dp, SIDE), lax.rem(dp, SIDE), lax.div(et, 2), lax.rem(et, 2)


def turn(value, by):
    return lax.rem(value + by, SIDE)


def device(y, z, x, c):
    return (y * SIDE + z, x * 2 + c)


def remote(src, dst, send_sem, recv_sem, target):
    return pltpu.make_async_remote_copy(
        src_ref=src, dst_ref=dst, send_sem=send_sem, recv_sem=recv_sem, device_id=target, device_id_type=MESH
    )


def greet(y, z, x, c):
    barrier = pltpu.get_barrier_semaphore()
    others = [device(y, z, x, 1 - c)]
    others += [device(y, z, turn(x, 1), c), device(y, z, turn(x, 3), c)]
    others += [device(y, turn(z, 1), x, c), device(y, turn(z, 3), x, c)]
    others += [device(turn(y, by), z, x, c) for by in (1, 2, 3)]
    for other in others:
        pl.semaphore_signal(barrier, inc=1, device_id=other, device_id_type=MESH)
    pl.semaphore_wait(barrier, len(others))


def halves_below(value):
    return jnp.concatenate([value[:, :PART], value[:, PART:]], axis=0)


def pack_rows(routes, probs, tok, cot, pack):
    count = tok.shape[0]
    slots = (CAP, count)
    route = routes[...].astype(F32)
    prob = probs[...]
    r0 = jnp.broadcast_to(route[0:1], slots)
    r1 = jnp.broadcast_to(route[1:2], slots)
    p0 = jnp.broadcast_to(prob[0:1], slots)
    p1 = jnp.broadcast_to(prob[1:2], slots)
    square = (count, count)
    first = lax.broadcasted_iota(jnp.int32, square, 0)
    second = lax.broadcasted_iota(jnp.int32, square, 1)
    before = jnp.where(first < second, 1.0, 0.0).astype(BF16)
    slot = lax.broadcasted_iota(jnp.int32, slots, 0).astype(F32)
    x_all = tok[...]
    d_all = cot[...]
    for e in range(EXP):
        in0 = jnp.where(r0 == e, 1.0, 0.0)
        in1 = jnp.where(r1 == e, 1.0, 0.0)
        member = in0 + in1
        placed = jnp.dot(member.astype(BF16), before, preferred_element_type=F32)
        pick = jnp.where(placed == slot, member, 0.0)
        weight = jnp.sum(pick * (in0 * p0 + in1 * p1), axis=1, keepdims=True)
        pick = pick.astype(BF16)
        chosen = jnp.dot(pick, x_all, preferred_element_type=F32)
        scaled = weight * jnp.dot(pick, d_all, preferred_element_type=F32)
        pack[0, e] = halves_below(chosen).astype(BF16)
        pack[1, e] = halves_below(scaled).astype(BF16)


def main_kernel(
    routes, probs, tok, cot, wg, wu, wd, xg, sg, h_out, dg_out, du_out, back_out,
    pack, recv, xb, sb, wgv, wuv, wdv, acc_g, acc_u, acc_d, hb, dgb, dub,
    own, precv, far, farr, mid, midr, far2, far2r, mid2, mid2r, first_sum, ysend, yrecv,
    w_sem, out_sem, ys, yr, n1s, n1r, h1s, h1r, n2s, n2r, h2s, h2r, ps, pr,
    qs, qr, fs, fr, ms, mr, f2s, f2r, m2s, m2r, bs, br,
):
    y, z, x, c = place()
    for i, (src, dst) in enumerate(((wg, wgv), (wu, wuv), (wd, wdv))):
        for k in range(ETS):
            pltpu.make_async_copy(src.at[:, pl.ds(k * WIDE, WIDE)], dst.at[k], w_sem.at[i, k]).start()

    def weights_here(i):
        src, dst = ((wg, wgv), (wu, wuv), (wd, wdv))[i]
        for k in range(ETS):
            pltpu.make_async_copy(src.at[:, pl.ds(k * WIDE, WIDE)], dst.at[k], w_sem.at[i, k]).wait()

    pack_rows(routes, probs, tok, cot, pack)
    greet(y, z, x, c)

    def y_copy(a, by, slot_from, slot_to, target):
        return remote(pack.at[a, slot_from], recv.at[a, slot_to], ys.at[a, by - 1], yr.at[a, by - 1], device(target, z, x, c))

    for a in (0, 1):
        for by in (1, 2, 3):
            e = turn(y, by)
            y_copy(a, by, e, y, e).start()

    bufs = (xb, sb)
    own_et = x * 2 + c
    partner = device(y, z, x, 1 - c)
    low, high = pl.ds(0, HALF), pl.ds(HALF, HALF)

    def assemble(a):
        recv[a, y] = pack[a, y]
        for by in (1, 2, 3):
            source = turn(y, SIDE - by)
            y_copy(a, by, source, source, source).wait_recv()
        parts = [recv[a, i].astype(F32) for i in range(SIDE)]
        for h in FLOWS:
            piece = [part[h * CAP:(h + 1) * CAP] for part in parts]
            bufs[a][z, own_et * 2 + h] = jnp.concatenate(piece, axis=0).astype(BF16)

    def chunk(a, h, first, second, core):
        if h == 0:
            return bufs[a].at[second, (first * 2 + core) * 2]
        return bufs[a].at[first, (second * 2 + core) * 2 + 1]

    def mine(h):
        return (x, z) if h == 0 else (z, x)

    def on_x(by):
        return device(y, z, turn(x, by), c)

    def on_z(by):
        return device(y, turn(z, by), x, c)

    def first_dev(h, by):
        return on_x(by) if h == 0 else on_z(by)

    def second_dev(h, by):
        return on_z(by) if h == 0 else on_x(by)

    GO = (1, 3)
    COME = (3, 1)

    def swap_copy(a, h, i, j, core):
        f, s = mine(h)
        ref = chunk(a, h, turn(f, j), turn(s, i), core)
        return remote(ref, ref, ps.at[a, h, i, j], pr.at[a, h, i, j], partner)

    def to_partner(a, h, i, j):
        swap_copy(a, h, i, j, c).start()

    def from_partner(a):
        def one(n, carry):
            for h in FLOWS:
                swap_copy(a, h, lax.div(n, SIDE), lax.rem(n, SIDE), 1 - c).wait_recv()
            return carry

        lax.fori_loop(0, SIDE * SIDE, one, 0)

    def first_full(a, h, d, by):
        f, s = mine(h)
        ref = chunk(a, h, turn(f, by), s, c)
        return ref, remote(ref, ref, n1s.at[a, h, d], n1r.at[a, h, d], first_dev(h, GO[d]))

    def first_half(a, h, d, by):
        f, s = mine(h)
        ref = chunk(a, h, turn(f, by), s, c).at[low if d == 0 else high]
        return remote(ref, ref, h1s.at[a, h, d], h1r.at[a, h, d], first_dev(h, GO[d]))

    def second_full(a, h, j, d, by):
        f, s = mine(h)
        ref = chunk(a, h, turn(f, j), turn(s, by), c)
        return remote(ref, ref, n2s.at[a, h, j, d], n2r.at[a, h, j, d], second_dev(h, GO[d]))

    def second_half(a, h, j, d, by):
        f, s = mine(h)
        ref = chunk(a, h, turn(f, j), turn(s, by), c).at[low if d == 0 else high]
        return remote(ref, ref, h2s.at[a, h, j, d], h2r.at[a, h, j, d], second_dev(h, GO[d]))

    def first_send(a):
        for d in (0, 1):
            for h in FLOWS:
                first_full(a, h, d, 0)[1].start()

    def second_send(a, j):
        for d in (0, 1):
            for h in FLOWS:
                second_full(a, h, j, d, 0).start()
        for h in FLOWS:
            to_partner(a, h, 0, j)

    def first_recv(a, d):
        for h in FLOWS:
            first_full(a, h, d, COME[d])[1].wait_recv()
            first_half(a, h, d, COME[d]).start()
        second_send(a, COME[d])

    def first_far(a):
        for h in FLOWS:
            for d in (0, 1):
                first_half(a, h, d, 2).wait_recv()
        second_send(a, 2)

    def second_recv(a, j):
        for d in (0, 1):
            for h in FLOWS:
                second_full(a, h, j, d, COME[d]).wait_recv()
                second_half(a, h, j, d, COME[d]).start()
                to_partner(a, h, COME[d], j)

    def second_far(a, j):
        for h in FLOWS:
            for d in (0, 1):
                second_half(a, h, j, d, 2).wait_recv()
            to_partner(a, h, 2, j)

    def gather_sent(a):
        for h in FLOWS:
            for d in (0, 1):
                first_full(a, h, d, 0)[1].wait_send()
                first_half(a, h, d, COME[d]).wait_send()

            def one(n, carry, h=h):
                swap_copy(a, h, lax.div(n, SIDE), lax.rem(n, SIDE), c).wait_send()
                return carry

            lax.fori_loop(0, SIDE * SIDE, one, 0)

            def ring(j, carry, h=h):
                for d in (0, 1):
                    second_full(a, h, j, d, 0).wait_send()
                    second_half(a, h, j, d, COME[d]).wait_send()
                return carry

            lax.fori_loop(0, SIDE, ring, 0)

    def rows_of(buf, k):
        left = buf[:, k * 2].reshape(ALL_ROWS, PART)
        right = buf[:, k * 2 + 1].reshape(ALL_ROWS, PART)
        return jnp.concatenate([left, right], axis=1)

    def gate_up(k0, k1):
        def step(k, carry):
            rows = rows_of(xb, k)
            acc_g[...] += lax.dot_general(rows, wgv[k], NT, preferred_element_type=F32)
            acc_u[...] += lax.dot_general(rows, wuv[k], NT, preferred_element_type=F32)
            return carry

        lax.fori_loop(k0, k1, step, 0)

    def d_hidden(k0, k1):
        def step(k, carry):
            acc_d[...] += lax.dot_general(rows_of(sb, k), wdv[k], NT, preferred_element_type=F32)
            return carry

        lax.fori_loop(k0, k1, step, 0)

    def activate():
        def step(i, carry):
            rows = pl.ds(pl.multiple_of(i * 32, 32), 32)
            gate = acc_g[rows, :]
            up = acc_u[rows, :]
            squash = jax.nn.sigmoid(gate)
            active = gate * squash
            hb[rows, :] = (active * up).astype(BF16)
            acc_g[rows, :] = up * squash * (1.0 + gate * (1.0 - squash))
            acc_u[rows, :] = active
            return carry

        lax.fori_loop(0, ALL_ROWS // 32, step, 0)

    def activate_back():
        def step(i, carry):
            rows = pl.ds(pl.multiple_of(i * 32, 32), 32)
            back = acc_d[rows, :]
            dgb[rows, :] = (back * acc_g[rows, :]).astype(BF16)
            dub[rows, :] = (back * acc_u[rows, :]).astype(BF16)
            return carry

        lax.fori_loop(0, ALL_ROWS // 32, step, 0)

    def give(b, h, sl):
        return xb.at[sl, pl.ds((b * 2 + h) * SIDE, SIDE)]

    def pair_copy(b, h, j):
        sl = turn(x if h == 0 else z, j)
        return remote(give(b, h, sl), precv.at[b, h, sl], qs.at[b, h, j], qr.at[b, h, j], partner)

    def keep_and_give(b, j):
        at = turn(x, j)

        def product(core):
            if b == 0:
                return jnp.dot(hb[...], wdv[at * 2 + core], preferred_element_type=F32)
            out = jnp.dot(dgb[...], wgv[at * 2 + core], preferred_element_type=F32)
            return out + jnp.dot(dub[...], wuv[at * 2 + core], preferred_element_type=F32)

        stacked = (SIDE, ROWS, PART)
        other = product(1 - c).astype(BF16)
        xb[at, pl.ds(b * 2 * SIDE, SIDE)] = other[:, :PART].reshape(stacked)
        xb[:, (b * 2 + 1) * SIDE + at] = other[:, PART:].reshape(stacked)
        pair_copy(b, 0, j).start()
        keep = product(c)
        own[b, 0, at] = keep[:, :PART].reshape(stacked)
        own[b, 1, :, at] = keep[:, PART:].reshape(stacked)

    def give_rest(b):
        for j in (2, 3, 1, 0):
            pair_copy(b, 1, j).start()

    def ring1(h, by):
        return on_z(by) if h == 0 else on_x(by)

    def ring2(h, by):
        return on_x(by) if h == 0 else on_z(by)

    def pair_sum(b, h, j, by):
        sl = turn(x if h == 0 else z, j)
        fi = turn(z if h == 0 else x, by)
        return own[b, h, sl, fi] + precv[b, h, sl, fi].astype(F32)

    def far_copy(b, h, j, d):
        part = high if d == 0 else low
        return remote(far.at[b, h, j, part], farr.at[b, h, j, d], fs.at[b, h, j, d], fr.at[b, h, j, d], ring1(h, GO[d]))

    def send_far(b, h, j):
        pair_copy(b, h, j).wait_recv()
        far[b, h, j] = pair_sum(b, h, j, 2).astype(BF16)
        for d in (0, 1):
            far_copy(b, h, j, d).start()

    def mid_copy(b, h, j, d):
        return remote(mid.at[b, h, j, d], midr.at[b, h, j, d], ms.at[b, h, j, d], mr.at[b, h, j, d], ring1(h, GO[d]))

    def add_half(total, part, d):
        if d == 0:
            return jnp.concatenate([total[:HALF], total[HALF:] + part], axis=0)
        return jnp.concatenate([total[:HALF] + part, total[HALF:]], axis=0)

    def send_mid(b, j):
        for d in (0, 1):
            for h in FLOWS:
                total = pair_sum(b, h, j, GO[d])
                far_copy(b, h, j, d).wait_recv()
                total = add_half(total, farr[b, h, j, d].astype(F32), d)
                mid[b, h, j, d] = total.astype(BF16)
                mid_copy(b, h, j, d).start()

    def finish_first(b, h, j):
        total = pair_sum(b, h, j, 0)
        for d in (0, 1):
            mid_copy(b, h, j, d).wait_recv()
            total = total + midr[b, h, j, d].astype(F32)
        first_sum[b, h, j] = total

    def far2_copy(b, h, d):
        part = high if d == 0 else low
        return remote(far2.at[b, h, part], far2r.at[b, h, d], f2s.at[b, h, d], f2r.at[b, h, d], ring2(h, GO[d]))

    def mid2_copy(b, h, d):
        return remote(mid2.at[b, h, d], mid2r.at[b, h, d], m2s.at[b, h, d], m2r.at[b, h, d], ring2(h, GO[d]))

    def send_far2(b):
        for h in FLOWS:
            finish_first(b, h, 2)
            far2[b, h] = first_sum[b, h, 2].astype(BF16)
            for d in (0, 1):
                far2_copy(b, h, d).start()

    def send_mid2(b, d):
        for h in FLOWS:
            finish_first(b, h, GO[d])
            total = first_sum[b, h, GO[d]]
            far2_copy(b, h, d).wait_recv()
            total = add_half(total, far2r[b, h, d].astype(F32), d)
            mid2[b, h, d] = total.astype(BF16)
            mid2_copy(b, h, d).start()

    def back_copy(b, by, slot_from, slot_to, target):
        return remote(ysend.at[b, slot_from], yrecv.at[b, slot_to], bs.at[b, by - 1], br.at[b, by - 1], device(target, z, x, c))

    def send_back(b):
        totals = []
        for h in FLOWS:
            finish_first(b, h, 0)
            total = first_sum[b, h, 0]
            for d in (0, 1):
                mid2_copy(b, h, d).wait_recv()
                total = total + mid2r[b, h, d].astype(F32)
            totals.append(total)
        for i in range(SIDE):
            piece = [total[i * CAP:(i + 1) * CAP] for total in totals]
            ysend[b, i] = jnp.concatenate(piece, axis=0).astype(BF16)
        for by in (1, 2, 3):
            target = turn(y, by)
            back_copy(b, by, target, y, target).start()
        yrecv[b, y] = ysend[b, y]

    def back_here(b):
        for by in (1, 2, 3):
            source = turn(y, SIDE - by)
            back_copy(b, by, source, source, source).wait_recv()
        back_out[b] = yrecv[b]

    assemble(0)
    first_send(0)
    second_send(0, 0)
    acc_g[...] = jnp.zeros_like(acc_g)
    acc_u[...] = jnp.zeros_like(acc_u)
    acc_d[...] = jnp.zeros_like(acc_d)
    assemble(1)
    first_recv(0, 0)
    first_recv(0, 1)
    second_recv(0, 0)
    first_far(0)
    second_recv(0, 3)
    first_send(1)
    second_send(1, 0)
    second_far(0, 0)
    second_recv(0, 1)
    second_far(0, 3)
    second_recv(0, 2)
    second_far(0, 1)
    first_recv(1, 0)
    first_recv(1, 1)
    second_far(0, 2)
    from_partner(0)
    out_x = pltpu.make_async_copy(xb, xg, out_sem.at[0])
    out_x.start()
    weights_here(0)
    weights_here(1)
    gate_up(0, 2)
    second_recv(1, 0)
    first_far(1)
    gate_up(2, 5)
    second_recv(1, 3)
    second_far(1, 0)
    gate_up(5, 8)
    activate()
    second_recv(1, 1)
    second_far(1, 3)
    gather_sent(0)
    out_x.wait()
    weights_here(2)
    keep_and_give(0, 2)
    keep_and_give(0, 3)
    second_recv(1, 2)
    second_far(1, 1)
    send_far(0, 0, 2)
    keep_and_give(0, 1)
    send_far(0, 0, 3)
    keep_and_give(0, 0)
    give_rest(0)
    send_far(0, 0, 1)
    second_far(1, 2)
    send_far(0, 1, 2)
    send_far(0, 1, 3)
    send_far(0, 0, 0)
    send_far(0, 1, 1)
    send_far(0, 1, 0)
    from_partner(1)
    out_s = pltpu.make_async_copy(sb, sg, out_sem.at[1])
    out_s.start()
    d_hidden(0, 3)
    send_mid(0, 2)
    d_hidden(3, 6)
    send_mid(0, 3)
    d_hidden(6, 8)
    activate_back()
    send_mid(0, 1)
    keep_and_give(1, 2)
    send_mid(0, 0)
    keep_and_give(1, 3)
    send_far2(0)
    send_far(1, 0, 2)
    keep_and_give(1, 1)
    send_far(1, 0, 3)
    send_mid2(0, 1)
    keep_and_give(1, 0)
    give_rest(1)
    send_far(1, 0, 1)
    send_far(1, 1, 2)
    send_far(1, 1, 3)
    send_far(1, 0, 0)
    send_far(1, 1, 1)
    send_far(1, 1, 0)
    send_mid2(0, 0)
    h_out[...] = hb[...]
    dg_out[...] = dgb[...]
    du_out[...] = dub[...]
    send_mid(1, 2)
    send_mid(1, 3)
    send_back(0)
    send_mid(1, 1)
    send_mid(1, 0)
    send_far2(1)
    send_mid2(1, 1)
    send_mid2(1, 0)
    back_here(0)
    send_back(1)
    back_here(1)

    out_s.wait()
    gather_sent(1)
    for a in (0, 1):
        for by in (1, 2, 3):
            e = turn(y, by)
            y_copy(a, by, e, y, e).wait_send()
            back_copy(a, by, e, y, e).wait_send()
        for h in FLOWS:
            for d in (0, 1):
                far2_copy(a, h, d).wait_send()
                mid2_copy(a, h, d).wait_send()

            def drain(j, carry, a=a, h=h):
                pair_copy(a, h, j).wait_send()
                for d in (0, 1):
                    far_copy(a, h, j, d).wait_send()
                    mid_copy(a, h, j, d).wait_send()
                return carry

            lax.fori_loop(0, SIDE, drain, 0)


def spread_back(routes, probs, back, layer_out, token_out):
    count = layer_out.shape[0]
    square = (count, count)
    route = routes[...].astype(F32)
    prob = probs[...]
    r0 = jnp.transpose(jnp.broadcast_to(route[0:1], square))
    r1 = jnp.transpose(jnp.broadcast_to(route[1:2], square))
    p0 = jnp.transpose(jnp.broadcast_to(prob[0:1], square))[:, 0:1]
    p1 = jnp.transpose(jnp.broadcast_to(prob[1:2], square))[:, 0:1]
    first = lax.broadcasted_iota(jnp.int32, square, 0)
    second = lax.broadcasted_iota(jnp.int32, square, 1)
    before = jnp.where(second < first, 1.0, 0.0).astype(BF16)
    lane = second.astype(F32)
    layer = [jnp.zeros((count, PART), F32) for _ in FLOWS]
    token = [jnp.zeros((count, PART), F32) for _ in FLOWS]
    for e in range(EXP):
        in0 = jnp.where(r0 == e, 1.0, 0.0)
        in1 = jnp.where(r1 == e, 1.0, 0.0)
        member = in0 + in1
        placed = jnp.dot(before, member.astype(BF16), preferred_element_type=F32)
        weight = in0[:, 0:1] * p0 + in1[:, 0:1] * p1
        for h in FLOWS:
            pick = jnp.where(placed + h * CAP == lane, member, 0.0)
            pick = jnp.where((lane >= h * CAP) & (lane < (h + 1) * CAP), pick, 0.0)
            pick = pick[:, :2 * CAP].astype(BF16)
            layer[h] = layer[h] + weight * jnp.dot(pick, back[0, e], preferred_element_type=F32)
            token[h] = token[h] + jnp.dot(pick, back[1, e], preferred_element_type=F32)
    layer_out[...] = jnp.concatenate(layer, axis=1).astype(BF16)
    token_out[...] = jnp.concatenate(token, axis=1).astype(BF16)


def grads_kernel(
    routes, probs, back, xg, sg, h, dg, du, layer_out, token_out, gate_out, up_out, down_out, ht, dt
):
    units = gate_out.shape[0]

    @pl.when(pl.program_id(0) == 0)
    def _():
        ht[...] = jnp.transpose(h[...])
        dt[:units] = jnp.transpose(dg[...])
        dt[units:] = jnp.transpose(du[...])
        spread_back(routes, probs, back, layer_out, token_out)

    for i in FLOWS:
        columns = slice(i * PART, (i + 1) * PART)
        rows_x = xg[:, i].reshape(ALL_ROWS, PART)
        rows_s = sg[:, i].reshape(ALL_ROWS, PART)
        both = jnp.dot(dt[...], rows_x, preferred_element_type=F32).astype(BF16)
        gate_out[:, columns] = both[:units]
        up_out[:, columns] = both[units:]
        down_out[:, columns] = jnp.dot(ht[...], rows_s, preferred_element_type=F32).astype(BF16)


def per_device(tokens, routes, route_probs, grad_out, w_gate, w_up, w_down):
    units, width = w_gate.shape
    count = tokens.shape[0]
    vmem = pl.BlockSpec(memory_space=pltpu.VMEM)
    anywhere = pl.BlockSpec(memory_space=pl.ANY)
    dma = pltpu.SemaphoreType.DMA
    gathered = jax.ShapeDtypeStruct((SIDE, 2 * ETS, ROWS, PART), BF16)
    small = jax.ShapeDtypeStruct((ALL_ROWS, units), BF16)
    back_shape = jax.ShapeDtypeStruct((2, EXP, 2 * CAP, PART), BF16)
    weight_buf = pltpu.VMEM((ETS, units, WIDE), BF16)
    gather_buf = pltpu.VMEM((SIDE, 2 * ETS, ROWS, PART), BF16)
    acc = pltpu.VMEM((ALL_ROWS, units), F32)
    hidden_buf = pltpu.VMEM((ALL_ROWS, units), BF16)
    packed = pltpu.VMEM((2, EXP, 2 * CAP, PART), BF16)
    routes_t = routes.T
    probs_t = route_probs.T
    xg, sg, h, dg, du, back = pl.pallas_call(
        main_kernel,
        out_shape=(gathered, gathered, small, small, small, back_shape),
        in_specs=[vmem] * 4 + [anywhere] * 3,
        out_specs=(anywhere, anywhere, vmem, vmem, vmem, vmem),
        scratch_shapes=[
            packed, packed, gather_buf, gather_buf, weight_buf, weight_buf, weight_buf,
            acc, acc, acc, hidden_buf, hidden_buf, hidden_buf,
            pltpu.VMEM((2, 2, SIDE, SIDE, ROWS, PART), F32),
            pltpu.VMEM((2, 2, SIDE, SIDE, ROWS, PART), BF16),
            pltpu.VMEM((2, 2, SIDE, ROWS, PART), BF16),
            pltpu.VMEM((2, 2, SIDE, 2, HALF, PART), BF16),
            pltpu.VMEM((2, 2, SIDE, 2, ROWS, PART), BF16),
            pltpu.VMEM((2, 2, SIDE, 2, ROWS, PART), BF16),
            pltpu.VMEM((2, 2, ROWS, PART), BF16),
            pltpu.VMEM((2, 2, 2, HALF, PART), BF16),
            pltpu.VMEM((2, 2, 2, ROWS, PART), BF16),
            pltpu.VMEM((2, 2, 2, ROWS, PART), BF16),
            pltpu.VMEM((2, 2, SIDE, ROWS, PART), F32),
            packed, packed,
            dma((3, ETS)), dma((2,)), dma((2, 3)), dma((2, 3)),
            dma((2, 2, 2)), dma((2, 2, 2)), dma((2, 2, 2)), dma((2, 2, 2)),
            dma((2, 2, 4, 2)), dma((2, 2, 4, 2)), dma((2, 2, 4, 2)), dma((2, 2, 4, 2)),
            dma((2, 2, 4, 4)), dma((2, 2, 4, 4)),
            dma((2, 2, 4)), dma((2, 2, 4)),
            dma((2, 2, 4, 2)), dma((2, 2, 4, 2)), dma((2, 2, 4, 2)), dma((2, 2, 4, 2)),
            dma((2, 2, 2)), dma((2, 2, 2)), dma((2, 2, 2)), dma((2, 2, 2)),
            dma((2, 3)), dma((2, 3)),
        ],
        compiler_params=pltpu.CompilerParams(collective_id=0, has_side_effects=True, vmem_limit_bytes=VMEM_LIMIT),
        name="expert_layer",
    )(routes_t, probs_t, tokens, grad_out, w_gate, w_up, w_down)

    block = pl.BlockSpec((SIDE, 2, ROWS, PART), lambda k: (0, k, 0, 0))
    whole = pl.BlockSpec((ALL_ROWS, units), lambda k: (0, 0))
    route_spec = pl.BlockSpec(routes_t.shape, lambda k: (0, 0))
    token_spec = pl.BlockSpec(tokens.shape, lambda k: (0, 0))
    token_shape = jax.ShapeDtypeStruct(tokens.shape, BF16)
    grad_spec = pl.BlockSpec((units, WIDE), lambda k: (0, k))
    grad_shape = jax.ShapeDtypeStruct((units, width), BF16)
    return pl.pallas_call(
        grads_kernel,
        grid=(width // WIDE,),
        out_shape=(token_shape, token_shape, grad_shape, grad_shape, grad_shape),
        in_specs=[
            route_spec, route_spec, pl.BlockSpec(back_shape.shape, lambda k: (0, 0, 0, 0)),
            block, block, whole, whole, whole,
        ],
        out_specs=(token_spec, token_spec, grad_spec, grad_spec, grad_spec),
        scratch_shapes=[pltpu.VMEM((units, ALL_ROWS), BF16), pltpu.VMEM((2 * units, ALL_ROWS), BF16)],
        compiler_params=pltpu.CompilerParams(vmem_limit_bytes=VMEM_LIMIT),
        name="weight_grads",
    )(routes_t, probs_t, back, xg, sg, h, dg, du)


def solution(mesh):
    return jax.shard_map(
        per_device,
        mesh=mesh,
        in_specs=(
            P("dp", "et"),
            P("dp", None),
            P("dp", None),
            P("dp", "et"),
            P(("dp", "et"), None),
            P(("dp", "et"), None),
            P(("dp", "et"), None),
        ),
        out_specs=(
            P("dp", "et"),
            P("dp", "et"),
            P(("dp", "et"), None),
            P(("dp", "et"), None),
            P(("dp", "et"), None),
        ),
        check_vma=False,
    )
```

```python
import jax
import jax.numpy as jnp
from jax import lax
from jax.experimental import pallas as pl
from jax.experimental.pallas import tpu as pltpu
from jax.sharding import PartitionSpec as P

MESH = pl.DeviceIdType.MESH
EXP = 4
CAP = 40
SIDE = 4
ROWS = SIDE * CAP
ALL_ROWS = SIDE * ROWS
HALF = ROWS // 2
ETS = 8
WIDE = 512
PART = 256
F32 = jnp.float32
BF16 = jnp.bfloat16
NT = (((1,), (1,)), ((), ()))
FLOWS = (0, 1)
VMEM_LIMIT = 62 * 1024 * 1024


def place():
    dp = lax.axis_index("dp")
    et = lax.axis_index("et")
    return lax.div(dp, SIDE), lax.rem(dp, SIDE), lax.div(et, 2), lax.rem(et, 2)


def turn(value, by):
    return lax.rem(value + by, SIDE)


def device(y, z, x, c):
    return (y * SIDE + z, x * 2 + c)


def remote(src, dst, send_sem, recv_sem, target):
    return pltpu.make_async_remote_copy(
        src_ref=src, dst_ref=dst, send_sem=send_sem, recv_sem=recv_sem, device_id=target, device_id_type=MESH
    )


def greet(y, z, x, c):
    barrier = pltpu.get_barrier_semaphore()
    others = [device(y, z, x, 1 - c)]
    others += [device(y, z, turn(x, 1), c), device(y, z, turn(x, 3), c)]
    others += [device(y, turn(z, 1), x, c), device(y, turn(z, 3), x, c)]
    others += [device(turn(y, by), z, x, c) for by in (1, 2, 3)]
    for other in others:
        pl.semaphore_signal(barrier, inc=1, device_id=other, device_id_type=MESH)
    pl.semaphore_wait(barrier, len(others))


def halves_below(value):
    return jnp.concatenate([value[:, :PART], value[:, PART:]], axis=0)


def pack_rows(routes, probs, tok, cot, pack):
    count = tok.shape[0]
    slots = (CAP, count)
    route = routes[...].astype(F32)
    prob = probs[...]
    r0 = jnp.broadcast_to(route[0:1], slots)
    r1 = jnp.broadcast_to(route[1:2], slots)
    p0 = jnp.broadcast_to(prob[0:1], slots)
    p1 = jnp.broadcast_to(prob[1:2], slots)
    square = (count, count)
    first = lax.broadcasted_iota(jnp.int32, square, 0)
    second = lax.broadcasted_iota(jnp.int32, square, 1)
    before = jnp.where(first < second, 1.0, 0.0).astype(BF16)
    slot = lax.broadcasted_iota(jnp.int32, slots, 0).astype(F32)
    x_all = tok[...]
    d_all = cot[...]
    for e in range(EXP):
        in0 = jnp.where(r0 == e, 1.0, 0.0)
        in1 = jnp.where(r1 == e, 1.0, 0.0)
        member = in0 + in1
        placed = jnp.dot(member.astype(BF16), before, preferred_element_type=F32)
        pick = jnp.where(placed == slot, member, 0.0)
        weight = jnp.sum(pick * (in0 * p0 + in1 * p1), axis=1, keepdims=True)
        pick = pick.astype(BF16)
        chosen = jnp.dot(pick, x_all, preferred_element_type=F32)
        scaled = weight * jnp.dot(pick, d_all, preferred_element_type=F32)
        pack[0, e] = halves_below(chosen).astype(BF16)
        pack[1, e] = halves_below(scaled).astype(BF16)


def main_kernel(
    routes, probs, tok, cot, wg, wu, wd, gate_out, up_out, down_out, back_out,
    pack, recv, xb, sb, wgv, wuv, wdv, acc_g, acc_u, acc_d, hb, dgb, dub,
    own, psend, precv, far, farr, mid, midr, far2, far2r, mid2, mid2r, ysend, yrecv, ht, dt, stage_x, stage_s,
    w_sem, out_sem, ys, yr, n1r, h1r, n2r, h2r, ring_s, ps, pr, qs, qr, fr, mr, f2r, m2r, sum_s, bs, br,
):
    y, z, x, c = place()
    weights = ((wg, wgv), (wu, wuv), (wd, wdv))
    for i, (src, dst) in enumerate(weights):
        for k in range(ETS):
            pltpu.make_async_copy(src.at[:, pl.ds(k * WIDE, WIDE)], dst.at[k], w_sem.at[i]).start()

    def wait_bytes(ref, sem):
        pltpu.make_async_copy(ref, ref, sem).wait()

    pack_rows(routes, probs, tok, cot, pack)
    greet(y, z, x, c)

    for a in (0, 1):
        for by in (1, 2, 3):
            e = turn(y, by)
            remote(pack.at[a, e], recv.at[a, y], ys.at[a], yr.at[a], device(e, z, x, c)).start()

    bufs = (xb, sb)
    own_et = x * 2 + c
    partner = device(y, z, x, 1 - c)
    low, high = pl.ds(0, HALF), pl.ds(HALF, HALF)
    three = pl.ds(0, 3)

    def assemble(a):
        recv[a, y] = pack[a, y]
        wait_bytes(recv.at[a, three], yr.at[a])
        parts = [recv[a, i].astype(F32) for i in range(SIDE)]
        for h in FLOWS:
            piece = [part[h * CAP:(h + 1) * CAP] for part in parts]
            bufs[a][z, own_et * 2 + h] = jnp.concatenate(piece, axis=0).astype(BF16)

    def chunk(a, h, first, second):
        if h == 0:
            return bufs[a].at[second, (first * 2 + c) * 2]
        return bufs[a].at[first, (second * 2 + c) * 2 + 1]

    def mine(h):
        return (x, z) if h == 0 else (z, x)

    def on_x(by):
        return device(y, z, turn(x, by), c)

    def on_z(by):
        return device(y, turn(z, by), x, c)

    def first_dev(h, by):
        return on_x(by) if h == 0 else on_z(by)

    def second_dev(h, by):
        return on_z(by) if h == 0 else on_x(by)

    GO = (1, 3)
    COME = (3, 1)
    one_chunk = xb.at[0, 0]
    two_chunks = xb.at[0, pl.ds(0, 2)]

    def to_partner(a, h, i, j):
        f, s = mine(h)
        ref = chunk(a, h, turn(f, j), turn(s, i))
        remote(ref, ref, ps.at[a], pr.at[a], partner).start()

    def from_partner(a):
        wait_bytes(bufs[a].at[:, pl.ds(0, ETS)], pr.at[a])

    def first_send(a, h):
        f, s = mine(h)
        ref = chunk(a, h, f, s)
        for d in (0, 1):
            remote(ref, ref, ring_s.at[a], n1r.at[a, h], first_dev(h, GO[d])).start()

    def second_send(a, h, j):
        f, s = mine(h)
        ref = chunk(a, h, turn(f, j), s)
        for d in (0, 1):
            remote(ref, ref, ring_s.at[a], n2r.at[a, h, j], second_dev(h, GO[d])).start()
        to_partner(a, h, 0, j)

    def first_recv(a, h):
        f, s = mine(h)
        wait_bytes(two_chunks, n1r.at[a, h])
        for d in (0, 1):
            ref = chunk(a, h, turn(f, COME[d]), s).at[low if d == 0 else high]
            remote(ref, ref, ring_s.at[a], h1r.at[a, h], first_dev(h, GO[d])).start()
        second_send(a, h, 1)
        second_send(a, h, 3)

    def first_far(a, h):
        wait_bytes(one_chunk, h1r.at[a, h])
        second_send(a, h, 2)

    def second_recv(a, h, j):
        f, s = mine(h)
        wait_bytes(two_chunks, n2r.at[a, h, j])
        for d in (0, 1):
            ref = chunk(a, h, turn(f, j), turn(s, COME[d])).at[low if d == 0 else high]
            remote(ref, ref, ring_s.at[a], h2r.at[a, h, j], second_dev(h, GO[d])).start()
        for d in (0, 1):
            to_partner(a, h, COME[d], j)

    def second_far(a, h, j):
        wait_bytes(one_chunk, h2r.at[a, h, j])
        to_partner(a, h, 2, j)

    def rows_of(buf, k):
        left = buf[:, k * 2].reshape(ALL_ROWS, PART)
        right = buf[:, k * 2 + 1].reshape(ALL_ROWS, PART)
        return jnp.concatenate([left, right], axis=1)

    def gate_ready():
        wait_bytes(wgv, w_sem.at[0])
        wait_bytes(wuv, w_sem.at[1])
        wait_bytes(wdv, w_sem.at[2])

    def add_to(acc, value, k):
        if k == 0:
            acc[...] = value
        else:
            acc[...] += value

    def gate_up(k):
        rows = rows_of(xb, k)
        add_to(acc_g, lax.dot_general(rows, wgv[k], NT, preferred_element_type=F32), k)
        add_to(acc_u, lax.dot_general(rows, wuv[k], NT, preferred_element_type=F32), k)

    def d_hidden(k):
        add_to(acc_d, lax.dot_general(rows_of(sb, k), wdv[k], NT, preferred_element_type=F32), k)

    STEPS = ALL_ROWS // 64

    def activate(part):
        def step(i, carry):
            rows = pl.ds(pl.multiple_of(i * 32, 32), 32)
            gate = acc_g[rows, :]
            up = acc_u[rows, :]
            squash = jax.nn.sigmoid(gate)
            active = gate * squash
            hb[rows, :] = (active * up).astype(BF16)
            acc_g[rows, :] = up * squash * (1.0 + gate * (1.0 - squash))
            acc_u[rows, :] = active
            return carry

        lax.fori_loop(part * STEPS, (part + 1) * STEPS, step, 0)

    def activate_back(part):
        def step(i, carry):
            rows = pl.ds(pl.multiple_of(i * 32, 32), 32)
            back = acc_d[rows, :]
            dgb[rows, :] = (back * acc_g[rows, :]).astype(BF16)
            dub[rows, :] = (back * acc_u[rows, :]).astype(BF16)
            return carry

        lax.fori_loop(part * STEPS, (part + 1) * STEPS, step, 0)

    stacked = (SIDE, ROWS, PART)

    def give_ready(b):
        if b == 1:
            wait_bytes(psend, qs)

    def send_pair(b, h, j):
        sl = turn(x if h == 0 else z, j)
        remote(psend.at[h, sl], precv.at[b, h, sl], qs, qr.at[b, h, j], partner).start()

    def product(b, et):
        if b == 0:
            return jnp.dot(hb[...], wdv[et], preferred_element_type=F32)
        out = jnp.dot(dgb[...], wgv[et], preferred_element_type=F32)
        return out + jnp.dot(dub[...], wuv[et], preferred_element_type=F32)

    def give(b, j):
        at = turn(x, j)
        other = product(b, at * 2 + 1 - c).astype(BF16)
        psend[0, at] = other[:, :PART].reshape(stacked)
        psend[1, :, at] = other[:, PART:].reshape(stacked)
        send_pair(b, 0, j)

    def keep(b, j):
        at = turn(x, j)
        value = product(b, at * 2 + c)
        own[b, 0, at] = value[:, :PART].reshape(stacked)
        own[b, 1, :, at] = value[:, PART:].reshape(stacked)

    def give_rest(b):
        for j in (2, 3, 1, 0):
            send_pair(b, 1, j)

    def ring1(h, by):
        return on_z(by) if h == 0 else on_x(by)

    def ring2(h, by):
        return on_x(by) if h == 0 else on_z(by)

    def spot(h, j, by):
        return turn(x if h == 0 else z, j), turn(z if h == 0 else x, by)

    def pair_sum(b, h, j, by):
        sl, fi = spot(h, j, by)
        return own[b, h, sl, fi] + precv[b, h, sl, fi].astype(F32)

    def send_far(b, h, j):
        sl, fi = spot(h, j, 2)
        wait_bytes(precv.at[b, h, sl], qr.at[b, h, j])
        far[b, h, j] = pair_sum(b, h, j, 2).astype(BF16)
        for d, part in ((0, high), (1, low)):
            remote(far.at[b, h, j, part], farr.at[b, h, j, d], sum_s.at[b], fr.at[b, h, j], ring1(h, GO[d])).start()

    def add_half(total, part, d):
        if d == 0:
            return jnp.concatenate([total[:HALF], total[HALF:] + part], axis=0)
        return jnp.concatenate([total[:HALF] + part, total[HALF:]], axis=0)

    def send_mid(b, h, j):
        wait_bytes(farr.at[b, h, j], fr.at[b, h, j])
        for d in (0, 1):
            total = add_half(pair_sum(b, h, j, GO[d]), farr[b, h, j, d].astype(F32), d)
            mid[b, h, j, d] = total.astype(BF16)
            remote(mid.at[b, h, j, d], midr.at[b, h, j, d], sum_s.at[b], mr.at[b, h, j], ring1(h, GO[d])).start()

    def finish_first(b, h, j):
        wait_bytes(midr.at[b, h, j], mr.at[b, h, j])
        sl, fi = spot(h, j, 0)
        total = pair_sum(b, h, j, 0)
        own[b, h, sl, fi] = total + midr[b, h, j, 0].astype(F32) + midr[b, h, j, 1].astype(F32)

    def first_sum(b, h, j):
        sl, fi = spot(h, j, 0)
        return own[b, h, sl, fi]

    def send_far2(b, h):
        far2[b, h] = first_sum(b, h, 2).astype(BF16)
        for d, part in ((0, high), (1, low)):
            remote(far2.at[b, h, part], far2r.at[b, h, d], sum_s.at[b], f2r.at[b, h], ring2(h, GO[d])).start()

    def send_mid2(b, h):
        wait_bytes(far2r.at[b, h], f2r.at[b, h])
        for d in (0, 1):
            total = add_half(first_sum(b, h, GO[d]), far2r[b, h, d].astype(F32), d)
            mid2[b, h, d] = total.astype(BF16)
            remote(mid2.at[b, h, d], mid2r.at[b, h, d], sum_s.at[b], m2r.at[b, h], ring2(h, GO[d])).start()

    def send_back(b):
        totals = []
        for h in FLOWS:
            wait_bytes(mid2r.at[b, h], m2r.at[b, h])
            total = first_sum(b, h, 0) + mid2r[b, h, 0].astype(F32) + mid2r[b, h, 1].astype(F32)
            totals.append(total)
        for i in range(SIDE):
            piece = [total[i * CAP:(i + 1) * CAP] for total in totals]
            ysend[b, i] = jnp.concatenate(piece, axis=0).astype(BF16)
        for by in (1, 2, 3):
            target = turn(y, by)
            remote(ysend.at[b, target], yrecv.at[b, y], bs.at[b], br.at[b], device(target, z, x, c)).start()
        yrecv[b, y] = ysend[b, y]

    def back_here(b):
        wait_bytes(yrecv.at[b, three], br.at[b])
        back_out[b] = yrecv[b]

    UNITS = wg.shape[0]

    def grads_ready():
        ht[...] = jnp.transpose(hb[...])
        dt[pl.ds(0, UNITS), :] = jnp.transpose(dgb[...])
        dt[pl.ds(UNITS, UNITS), :] = jnp.transpose(dub[...])

    def grad_copy(k, i):
        columns = pl.ds(k * WIDE, WIDE)
        slot = k % 2
        src = stage_s.at[slot] if i == 2 else stage_x.at[slot, pl.ds(i * UNITS, UNITS)]
        dst = (gate_out, up_out, down_out)[i]
        return pltpu.make_async_copy(src, dst.at[:, columns], out_sem.at[i, slot])

    def grad_x(k):
        if k > 1:
            grad_copy(k - 2, 0).wait()
            grad_copy(k - 2, 1).wait()
        stage_x[k % 2] = jnp.dot(dt[...], rows_of(xb, k), preferred_element_type=F32).astype(BF16)
        grad_copy(k, 0).start()
        grad_copy(k, 1).start()

    def grad_s(k):
        if k > 1:
            grad_copy(k - 2, 2).wait()
        stage_s[k % 2] = jnp.dot(ht[...], rows_of(sb, k), preferred_element_type=F32).astype(BF16)
        grad_copy(k, 2).start()

    assemble(0)
    first_send(0, 1)
    first_send(0, 0)
    second_send(0, 0, 0)
    second_send(0, 1, 0)
    assemble(1)
    first_recv(0, 1)
    first_recv(0, 0)
    second_recv(0, 0, 0)
    second_recv(0, 1, 0)
    first_far(0, 1)
    second_recv(0, 1, 1)
    second_recv(0, 0, 1)
    second_recv(0, 1, 3)
    second_recv(0, 0, 3)
    first_far(0, 0)
    second_far(0, 0, 0)
    second_far(0, 1, 0)
    second_far(0, 0, 1)
    second_far(0, 0, 3)
    second_recv(0, 1, 2)
    second_far(0, 1, 1)
    second_recv(0, 0, 2)
    second_far(0, 1, 3)
    first_send(1, 0)
    first_send(1, 1)
    second_send(1, 0, 0)
    second_send(1, 1, 0)
    second_far(0, 1, 2)
    second_far(0, 0, 2)
    first_recv(1, 0)
    from_partner(0)
    gate_ready()
    first_recv(1, 1)
    gate_up(0)
    second_recv(1, 1, 0)
    gate_up(1)
    first_far(1, 0)
    second_recv(1, 0, 0)
    gate_up(2)
    gate_up(3)
    second_recv(1, 1, 1)
    second_recv(1, 0, 1)
    gate_up(4)
    gate_up(5)
    second_recv(1, 0, 3)
    first_far(1, 1)
    second_recv(1, 1, 3)
    second_far(1, 1, 0)
    gate_up(6)
    second_far(1, 1, 1)
    gate_up(7)
    second_recv(1, 0, 2)
    activate(0)
    second_far(1, 0, 0)
    activate(1)
    second_recv(1, 1, 2)
    second_far(1, 0, 1)
    give_ready(0)
    give(0, 2)
    second_far(1, 1, 3)
    keep(0, 2)
    second_far(1, 0, 3)
    give(0, 3)
    keep(0, 3)
    second_far(1, 0, 2)
    second_far(1, 1, 2)
    give(0, 1)
    send_far(0, 0, 2)
    keep(0, 1)
    give(0, 0)
    send_far(0, 0, 3)
    keep(0, 0)
    from_partner(1)
    give_rest(0)
    send_far(0, 0, 1)
    send_mid(0, 0, 2)
    send_far(0, 0, 0)
    d_hidden(0)
    send_mid(0, 0, 3)
    send_far(0, 1, 2)
    d_hidden(1)
    send_far(0, 1, 3)
    send_mid(0, 0, 1)
    send_far(0, 1, 1)
    send_far(0, 1, 0)
    d_hidden(2)
    d_hidden(3)
    finish_first(0, 0, 2)
    send_far2(0, 0)
    send_mid(0, 1, 2)
    send_mid(0, 1, 3)
    send_mid(0, 0, 0)
    d_hidden(4)
    send_mid(0, 1, 1)
    d_hidden(5)
    send_mid(0, 1, 0)
    finish_first(0, 0, 3)
    d_hidden(6)
    d_hidden(7)
    activate_back(0)
    activate_back(1)
    finish_first(0, 0, 1)
    send_mid2(0, 0)
    give_ready(1)
    give(1, 2)
    finish_first(0, 1, 2)
    send_far2(0, 1)
    keep(1, 2)
    finish_first(0, 0, 0)
    finish_first(0, 1, 3)
    give(1, 3)
    send_far(1, 0, 2)
    keep(1, 3)
    finish_first(0, 1, 1)
    send_mid2(0, 1)
    give(1, 1)
    send_mid(1, 0, 2)
    send_far(1, 0, 3)
    finish_first(0, 1, 0)
    keep(1, 1)
    give(1, 0)
    send_far(1, 0, 1)
    send_back(0)
    keep(1, 0)
    give_rest(1)
    finish_first(1, 0, 2)
    send_far2(1, 0)
    send_far(1, 0, 0)
    grads_ready()
    send_mid(1, 0, 3)
    send_far(1, 1, 2)
    back_here(0)
    send_far(1, 1, 3)
    send_far(1, 1, 1)
    send_mid(1, 0, 0)
    send_far(1, 1, 0)
    send_mid(1, 0, 1)
    grad_x(0)
    send_mid(1, 1, 2)
    send_mid(1, 1, 3)
    finish_first(1, 0, 3)
    grad_s(0)
    send_mid(1, 1, 1)
    grad_x(1)
    send_mid(1, 1, 0)
    finish_first(1, 0, 0)
    grad_s(1)
    finish_first(1, 0, 1)
    send_mid2(1, 0)
    finish_first(1, 1, 2)
    send_far2(1, 1)
    grad_x(2)
    grad_s(2)
    finish_first(1, 1, 3)
    grad_x(3)
    grad_s(3)
    finish_first(1, 1, 1)
    send_mid2(1, 1)
    grad_x(4)
    finish_first(1, 1, 0)
    grad_s(4)
    grad_x(5)
    grad_s(5)
    send_back(1)
    grad_x(6)
    grad_s(6)
    grad_x(7)
    grad_s(7)
    back_here(1)

    for k in (ETS - 2, ETS - 1):
        for i in range(3):
            grad_copy(k, i).wait()
    wait_bytes(psend, qs)
    for a in (0, 1):
        wait_bytes(pack.at[a, three], ys.at[a])
        wait_bytes(ysend.at[a, three], bs.at[a])
        wait_bytes(bufs[a].at[:, pl.ds(0, ETS)], ps.at[a])
        thirty = bufs[a].at[pl.ds(0, 2), pl.ds(0, 15)]
        wait_bytes(thirty, ring_s.at[a])
        wait_bytes(thirty, sum_s.at[a])


def spread_back(routes, probs, back, layer_out, token_out):
    count = layer_out.shape[0]
    square = (count, count)
    route = routes[...].astype(F32)
    prob = probs[...]
    r0 = jnp.transpose(jnp.broadcast_to(route[0:1], square))
    r1 = jnp.transpose(jnp.broadcast_to(route[1:2], square))
    p0 = jnp.transpose(jnp.broadcast_to(prob[0:1], square))[:, 0:1]
    p1 = jnp.transpose(jnp.broadcast_to(prob[1:2], square))[:, 0:1]
    first = lax.broadcasted_iota(jnp.int32, square, 0)
    second = lax.broadcasted_iota(jnp.int32, square, 1)
    before = jnp.where(second < first, 1.0, 0.0).astype(BF16)
    lane = second.astype(F32)
    layer = [jnp.zeros((count, PART), F32) for _ in FLOWS]
    token = [jnp.zeros((count, PART), F32) for _ in FLOWS]
    for e in range(EXP):
        in0 = jnp.where(r0 == e, 1.0, 0.0)
        in1 = jnp.where(r1 == e, 1.0, 0.0)
        member = in0 + in1
        placed = jnp.dot(before, member.astype(BF16), preferred_element_type=F32)
        weight = in0[:, 0:1] * p0 + in1[:, 0:1] * p1
        for h in FLOWS:
            pick = jnp.where(placed + h * CAP == lane, member, 0.0)
            pick = jnp.where((lane >= h * CAP) & (lane < (h + 1) * CAP), pick, 0.0)
            pick = pick[:, :2 * CAP].astype(BF16)
            layer[h] = layer[h] + weight * jnp.dot(pick, back[0, e], preferred_element_type=F32)
            token[h] = token[h] + jnp.dot(pick, back[1, e], preferred_element_type=F32)
    layer_out[...] = jnp.concatenate(layer, axis=1).astype(BF16)
    token_out[...] = jnp.concatenate(token, axis=1).astype(BF16)


def finish_kernel(routes, probs, back, gate_in, up_in, down_in, layer_out, token_out, gate_out, up_out, down_out, held, sem):
    pairs = ((gate_in, gate_out), (up_in, up_out), (down_in, down_out))
    blocks = 4
    rows = gate_in.shape[0] // blocks

    def move(i, k, way):
        part = pl.ds(k * rows, rows)
        src, dst = pairs[i]
        if way == 0:
            return pltpu.make_async_copy(src.at[part], held.at[i, part], sem.at[0, i, k])
        return pltpu.make_async_copy(held.at[i, part], dst.at[part], sem.at[1, i, k])

    steps = [(i, k) for i in range(3) for k in range(blocks)]
    for i, k in steps:
        move(i, k, 0).start()
    spread_back(routes, probs, back, layer_out, token_out)
    for i, k in steps:
        move(i, k, 0).wait()
        move(i, k, 1).start()
    for i, k in steps:
        move(i, k, 1).wait()


def per_device(tokens, routes, route_probs, grad_out, w_gate, w_up, w_down):
    units, width = w_gate.shape
    count = tokens.shape[0]
    vmem = pl.BlockSpec(memory_space=pltpu.VMEM)
    anywhere = pl.BlockSpec(memory_space=pl.ANY)
    dma = pltpu.SemaphoreType.DMA
    back_shape = jax.ShapeDtypeStruct((2, EXP, 2 * CAP, PART), BF16)
    weight_buf = pltpu.VMEM((ETS, units, WIDE), BF16)
    gather_buf = pltpu.VMEM((SIDE, 2 * ETS, ROWS, PART), BF16)
    acc = pltpu.VMEM((ALL_ROWS, units), F32)
    hidden_buf = pltpu.VMEM((ALL_ROWS, units), BF16)
    packed = pltpu.VMEM((2, EXP, 2 * CAP, PART), BF16)
    routes_t = routes.T
    probs_t = route_probs.T
    grad_shape = jax.ShapeDtypeStruct((units, width), BF16)
    gate, up, down, back = pl.pallas_call(
        main_kernel,
        out_shape=(grad_shape, grad_shape, grad_shape, back_shape),
        in_specs=[vmem] * 4 + [anywhere] * 3,
        out_specs=(anywhere, anywhere, anywhere, vmem),
        scratch_shapes=[
            packed, packed, gather_buf, gather_buf, weight_buf, weight_buf, weight_buf,
            acc, acc, acc, hidden_buf, hidden_buf, hidden_buf,
            pltpu.VMEM((2, 2, SIDE, SIDE, ROWS, PART), F32),
            pltpu.VMEM((2, SIDE, SIDE, ROWS, PART), BF16),
            pltpu.VMEM((2, 2, SIDE, SIDE, ROWS, PART), BF16),
            pltpu.VMEM((2, 2, SIDE, ROWS, PART), BF16),
            pltpu.VMEM((2, 2, SIDE, 2, HALF, PART), BF16),
            pltpu.VMEM((2, 2, SIDE, 2, ROWS, PART), BF16),
            pltpu.VMEM((2, 2, SIDE, 2, ROWS, PART), BF16),
            pltpu.VMEM((2, 2, ROWS, PART), BF16),
            pltpu.VMEM((2, 2, 2, HALF, PART), BF16),
            pltpu.VMEM((2, 2, 2, ROWS, PART), BF16),
            pltpu.VMEM((2, 2, 2, ROWS, PART), BF16),
            packed, packed,
            pltpu.VMEM((units, ALL_ROWS), BF16),
            pltpu.VMEM((2 * units, ALL_ROWS), BF16),
            pltpu.VMEM((2, 2 * units, WIDE), BF16),
            pltpu.VMEM((2, units, WIDE), BF16),
            dma((3,)), dma((3, 2)), dma((2,)), dma((2,)),
            dma((2, 2)), dma((2, 2)), dma((2, 2, 4)), dma((2, 2, 4)), dma((2,)), dma((2,)), dma((2,)),
            dma(()), dma((2, 2, 4)), dma((2, 2, 4)), dma((2, 2, 4)), dma((2, 2)), dma((2, 2)), dma((2,)),
            dma((2,)), dma((2,)),
        ],
        compiler_params=pltpu.CompilerParams(collective_id=0, has_side_effects=True, vmem_limit_bytes=VMEM_LIMIT),
        name="expert_layer",
    )(routes_t, probs_t, tokens, grad_out, w_gate, w_up, w_down)

    token_shape = jax.ShapeDtypeStruct(tokens.shape, BF16)
    return pl.pallas_call(
        finish_kernel,
        out_shape=(token_shape, token_shape, grad_shape, grad_shape, grad_shape),
        in_specs=[vmem] * 3 + [anywhere] * 3,
        out_specs=(vmem, vmem, anywhere, anywhere, anywhere),
        scratch_shapes=[pltpu.VMEM((3, units, width), BF16), dma((2, 3, 4))],
        compiler_params=pltpu.CompilerParams(vmem_limit_bytes=VMEM_LIMIT),
        name="finish",
    )(routes_t, probs_t, back, gate, up, down)


def solution(mesh):
    return jax.shard_map(
        per_device,
        mesh=mesh,
        in_specs=(
            P("dp", "et"),
            P("dp", None),
            P("dp", None),
            P("dp", "et"),
            P(("dp", "et"), None),
            P(("dp", "et"), None),
            P(("dp", "et"), None),
        ),
        out_specs=(
            P("dp", "et"),
            P("dp", "et"),
            P(("dp", "et"), None),
            P(("dp", "et"), None),
            P(("dp", "et"), None),
        ),
        check_vma=False,
    )
```

```python
import jax
import jax.numpy as jnp
from jax import lax
from jax.experimental import pallas as pl
from jax.experimental.pallas import tpu as pltpu
from jax.sharding import PartitionSpec as P

MESH = pl.DeviceIdType.MESH
EXP = 4
CAP = 40
SIDE = 4
ROWS = SIDE * CAP
ALL_ROWS = SIDE * ROWS
HALF = ROWS // 2
ETS = 8
WIDE = 512
PART = 256
F32 = jnp.float32
BF16 = jnp.bfloat16
NT = (((1,), (1,)), ((), ()))
FLOWS = (0, 1)
VMEM_LIMIT = 62 * 1024 * 1024


def place():
    dp = lax.axis_index("dp")
    et = lax.axis_index("et")
    return lax.div(dp, SIDE), lax.rem(dp, SIDE), lax.div(et, 2), lax.rem(et, 2)


def turn(value, by):
    return lax.rem(value + by, SIDE)


def device(y, z, x, c):
    return (y * SIDE + z, x * 2 + c)


def remote(src, dst, send_sem, recv_sem, target):
    return pltpu.make_async_remote_copy(
        src_ref=src, dst_ref=dst, send_sem=send_sem, recv_sem=recv_sem, device_id=target, device_id_type=MESH
    )


def greet(y, z, x, c):
    barrier = pltpu.get_barrier_semaphore()
    others = [device(y, z, x, 1 - c)]
    others += [device(y, z, turn(x, 1), c), device(y, z, turn(x, 3), c)]
    others += [device(y, turn(z, 1), x, c), device(y, turn(z, 3), x, c)]
    others += [device(turn(y, by), z, x, c) for by in (1, 2, 3)]
    for other in others:
        pl.semaphore_signal(barrier, inc=1, device_id=other, device_id_type=MESH)
    return lambda: pl.semaphore_wait(barrier, len(others))


def halves_below(value):
    return jnp.concatenate([value[:, :PART], value[:, PART:]], axis=0)


def pack_rows(routes, probs, tok, cot, pack):
    count = tok.shape[0]
    slots = (CAP, count)
    route = routes[...].astype(F32)
    prob = probs[...]
    r0 = jnp.broadcast_to(route[0:1], slots)
    r1 = jnp.broadcast_to(route[1:2], slots)
    p0 = jnp.broadcast_to(prob[0:1], slots)
    p1 = jnp.broadcast_to(prob[1:2], slots)
    square = (count, count)
    first = lax.broadcasted_iota(jnp.int32, square, 0)
    second = lax.broadcasted_iota(jnp.int32, square, 1)
    before = jnp.where(first < second, 1.0, 0.0).astype(BF16)
    slot = lax.broadcasted_iota(jnp.int32, slots, 0).astype(F32)
    x_all = tok[...]
    d_all = cot[...]
    for e in range(EXP):
        in0 = jnp.where(r0 == e, 1.0, 0.0)
        in1 = jnp.where(r1 == e, 1.0, 0.0)
        member = in0 + in1
        placed = jnp.dot(member.astype(BF16), before, preferred_element_type=F32)
        pick = jnp.where(placed == slot, member, 0.0)
        weight = jnp.sum(pick * (in0 * p0 + in1 * p1), axis=1, keepdims=True)
        pick = pick.astype(BF16)
        chosen = jnp.dot(pick, x_all, preferred_element_type=F32)
        scaled = weight * jnp.dot(pick, d_all, preferred_element_type=F32)
        pack[0, e] = halves_below(chosen).astype(BF16)
        pack[1, e] = halves_below(scaled).astype(BF16)


def main_kernel(
    routes, probs, tok, cot, wg, wu, wd, gate_out, up_out, down_out, back_out,
    pack, recv, xb, sb, wgv, wuv, wdv, acc_g, acc_u, acc_d, hb, dgb, dub,
    own, psend, precv, far, farr, mid, midr, far2, far2r, mid2, mid2r, ysend, yrecv, ht, dt, stage_x, stage_s,
    w_sem, out_sem, ys, yr, n1r, h1r, n2r, h2r, ring_s, ps, pr, qs, qr, fr, mr, f2r, m2r, sum_s, bs, br,
):
    y, z, x, c = place()
    weights = ((wg, wgv), (wu, wuv), (wd, wdv))
    for i, (src, dst) in enumerate(weights):
        for k in range(ETS):
            pltpu.make_async_copy(src.at[:, pl.ds(k * WIDE, WIDE)], dst.at[k], w_sem.at[i]).start()

    def wait_bytes(ref, sem):
        pltpu.make_async_copy(ref, ref, sem).wait()

    await_greetings = greet(y, z, x, c)
    pack_rows(routes, probs, tok, cot, pack)
    await_greetings()

    for a in (0, 1):
        for by in (1, 2, 3):
            e = turn(y, by)
            remote(pack.at[a, e], recv.at[a, y], ys.at[a], yr.at[a], device(e, z, x, c)).start()

    bufs = (xb, sb)
    own_et = x * 2 + c
    partner = device(y, z, x, 1 - c)
    low, high = pl.ds(0, HALF), pl.ds(HALF, HALF)
    three = pl.ds(0, 3)

    def assemble(a):
        recv[a, y] = pack[a, y]
        wait_bytes(recv.at[a, three], yr.at[a])
        parts = [recv[a, i].astype(F32) for i in range(SIDE)]
        for h in FLOWS:
            piece = [part[h * CAP:(h + 1) * CAP] for part in parts]
            bufs[a][z, own_et * 2 + h] = jnp.concatenate(piece, axis=0).astype(BF16)

    def chunk(a, h, first, second):
        if h == 0:
            return bufs[a].at[second, (first * 2 + c) * 2]
        return bufs[a].at[first, (second * 2 + c) * 2 + 1]

    def mine(h):
        return (x, z) if h == 0 else (z, x)

    def on_x(by):
        return device(y, z, turn(x, by), c)

    def on_z(by):
        return device(y, turn(z, by), x, c)

    def first_dev(h, by):
        return on_x(by) if h == 0 else on_z(by)

    def second_dev(h, by):
        return on_z(by) if h == 0 else on_x(by)

    GO = (1, 3)
    COME = (3, 1)
    one_chunk = xb.at[0, 0]
    two_chunks = xb.at[0, pl.ds(0, 2)]

    def to_partner(a, h, i, j):
        f, s = mine(h)
        ref = chunk(a, h, turn(f, j), turn(s, i))
        remote(ref, ref, ps.at[a], pr.at[a, j if h == 0 else i], partner).start()

    def from_partner(a, group):
        wait_bytes(bufs[a].at[0, pl.ds(0, ETS)], pr.at[a, group])

    def first_send(a, h):
        f, s = mine(h)
        ref = chunk(a, h, f, s)
        for d in (0, 1):
            remote(ref, ref, ring_s.at[a], n1r.at[a, h], first_dev(h, GO[d])).start()

    def second_send(a, h, j):
        f, s = mine(h)
        ref = chunk(a, h, turn(f, j), s)
        for d in (0, 1):
            remote(ref, ref, ring_s.at[a], n2r.at[a, h, j], second_dev(h, GO[d])).start()
        to_partner(a, h, 0, j)

    def first_recv(a, h):
        f, s = mine(h)
        wait_bytes(two_chunks, n1r.at[a, h])
        for d in (0, 1):
            ref = chunk(a, h, turn(f, COME[d]), s).at[low if d == 0 else high]
            remote(ref, ref, ring_s.at[a], h1r.at[a, h], first_dev(h, GO[d])).start()
        second_send(a, h, 1)
        second_send(a, h, 3)

    def first_far(a, h):
        wait_bytes(one_chunk, h1r.at[a, h])
        second_send(a, h, 2)

    def second_recv(a, h, j):
        f, s = mine(h)
        wait_bytes(two_chunks, n2r.at[a, h, j])
        for d in (0, 1):
            ref = chunk(a, h, turn(f, j), turn(s, COME[d])).at[low if d == 0 else high]
            remote(ref, ref, ring_s.at[a], h2r.at[a, h, j], second_dev(h, GO[d])).start()
        for d in (0, 1):
            to_partner(a, h, COME[d], j)

    def second_far(a, h, j):
        wait_bytes(one_chunk, h2r.at[a, h, j])
        to_partner(a, h, 2, j)

    def rows_of(buf, k):
        left = buf[:, k * 2].reshape(ALL_ROWS, PART)
        right = buf[:, k * 2 + 1].reshape(ALL_ROWS, PART)
        return jnp.concatenate([left, right], axis=1)

    def gate_ready():
        wait_bytes(wgv, w_sem.at[0])
        wait_bytes(wuv, w_sem.at[1])
        wait_bytes(wdv, w_sem.at[2])

    def add_to(acc, value, first):
        if first:
            acc[...] = value
        else:
            acc[...] += value

    def gate_up(group, core):
        k = turn(x, group) * 2 + core
        first = group == 0 and core == 0
        rows = rows_of(xb, k)
        add_to(acc_g, lax.dot_general(rows, wgv[k], NT, preferred_element_type=F32), first)
        add_to(acc_u, lax.dot_general(rows, wuv[k], NT, preferred_element_type=F32), first)

    def d_hidden(group, core):
        k = turn(x, group) * 2 + core
        first = group == 0 and core == 0
        add_to(acc_d, lax.dot_general(rows_of(sb, k), wdv[k], NT, preferred_element_type=F32), first)

    STEPS = ALL_ROWS // 64

    def activate(part):
        def step(i, carry):
            rows = pl.ds(pl.multiple_of(i * 32, 32), 32)
            gate = acc_g[rows, :]
            up = acc_u[rows, :]
            squash = jax.nn.sigmoid(gate)
            active = gate * squash
            hb[rows, :] = (active * up).astype(BF16)
            acc_g[rows, :] = up * squash * (1.0 + gate * (1.0 - squash))
            acc_u[rows, :] = active
            return carry

        lax.fori_loop(part * STEPS, (part + 1) * STEPS, step, 0)

    def activate_back(part):
        def step(i, carry):
            rows = pl.ds(pl.multiple_of(i * 32, 32), 32)
            back = acc_d[rows, :]
            dgb[rows, :] = (back * acc_g[rows, :]).astype(BF16)
            dub[rows, :] = (back * acc_u[rows, :]).astype(BF16)
            return carry

        lax.fori_loop(part * STEPS, (part + 1) * STEPS, step, 0)

    stacked = (SIDE, ROWS, PART)

    def give_ready(b):
        if b == 1:
            wait_bytes(psend, qs)

    def send_pair(b, h, j):
        sl = turn(x if h == 0 else z, j)
        remote(psend.at[h, sl], precv.at[b, h, sl], qs, qr.at[b, h, j], partner).start()

    def product(b, et):
        if b == 0:
            return jnp.dot(hb[...], wdv[et], preferred_element_type=F32)
        out = jnp.dot(dgb[...], wgv[et], preferred_element_type=F32)
        return out + jnp.dot(dub[...], wuv[et], preferred_element_type=F32)

    def give(b, j):
        at = turn(x, j)
        other = product(b, at * 2 + 1 - c).astype(BF16)
        psend[0, at] = other[:, :PART].reshape(stacked)
        psend[1, :, at] = other[:, PART:].reshape(stacked)
        send_pair(b, 0, j)

    def keep(b, j):
        at = turn(x, j)
        value = product(b, at * 2 + c)
        own[b, 0, at] = value[:, :PART].reshape(stacked)
        own[b, 1, :, at] = value[:, PART:].reshape(stacked)

    def give_rest(b):
        for j in (2, 3, 1, 0):
            send_pair(b, 1, j)

    def ring1(h, by):
        return on_z(by) if h == 0 else on_x(by)

    def ring2(h, by):
        return on_x(by) if h == 0 else on_z(by)

    def spot(h, j, by):
        return turn(x if h == 0 else z, j), turn(z if h == 0 else x, by)

    def pair_sum(b, h, j, by):
        sl, fi = spot(h, j, by)
        return own[b, h, sl, fi] + precv[b, h, sl, fi].astype(F32)

    def send_far(b, h, j):
        sl, fi = spot(h, j, 2)
        wait_bytes(precv.at[b, h, sl], qr.at[b, h, j])
        far[b, h, j] = pair_sum(b, h, j, 2).astype(BF16)
        for d, part in ((0, high), (1, low)):
            remote(far.at[b, h, j, part], farr.at[b, h, j, d], sum_s.at[b], fr.at[b, h, j], ring1(h, GO[d])).start()

    def add_half(total, part, d):
        if d == 0:
            return jnp.concatenate([total[:HALF], total[HALF:] + part], axis=0)
        return jnp.concatenate([total[:HALF] + part, total[HALF:]], axis=0)

    def send_mid(b, h, j):
        wait_bytes(farr.at[b, h, j], fr.at[b, h, j])
        for d in (0, 1):
            total = add_half(pair_sum(b, h, j, GO[d]), farr[b, h, j, d].astype(F32), d)
            mid[b, h, j, d] = total.astype(BF16)
            remote(mid.at[b, h, j, d], midr.at[b, h, j, d], sum_s.at[b], mr.at[b, h, j], ring1(h, GO[d])).start()

    def finish_first(b, h, j):
        wait_bytes(midr.at[b, h, j], mr.at[b, h, j])
        sl, fi = spot(h, j, 0)
        total = pair_sum(b, h, j, 0)
        own[b, h, sl, fi] = total + midr[b, h, j, 0].astype(F32) + midr[b, h, j, 1].astype(F32)

    def first_sum(b, h, j):
        sl, fi = spot(h, j, 0)
        return own[b, h, sl, fi]

    def send_far2(b, h):
        far2[b, h] = first_sum(b, h, 2).astype(BF16)
        for d, part in ((0, high), (1, low)):
            remote(far2.at[b, h, part], far2r.at[b, h, d], sum_s.at[b], f2r.at[b, h], ring2(h, GO[d])).start()

    def send_mid2(b, h):
        wait_bytes(far2r.at[b, h], f2r.at[b, h])
        for d in (0, 1):
            total = add_half(first_sum(b, h, GO[d]), far2r[b, h, d].astype(F32), d)
            mid2[b, h, d] = total.astype(BF16)
            remote(mid2.at[b, h, d], mid2r.at[b, h, d], sum_s.at[b], m2r.at[b, h], ring2(h, GO[d])).start()

    def send_back(b):
        totals = []
        for h in FLOWS:
            wait_bytes(mid2r.at[b, h], m2r.at[b, h])
            total = first_sum(b, h, 0) + mid2r[b, h, 0].astype(F32) + mid2r[b, h, 1].astype(F32)
            totals.append(total)
        for i in range(SIDE):
            piece = [total[i * CAP:(i + 1) * CAP] for total in totals]
            ysend[b, i] = jnp.concatenate(piece, axis=0).astype(BF16)
        for by in (1, 2, 3):
            target = turn(y, by)
            remote(ysend.at[b, target], yrecv.at[b, y], bs.at[b], br.at[b], device(target, z, x, c)).start()
        yrecv[b, y] = ysend[b, y]

    def back_here(b):
        wait_bytes(yrecv.at[b, three], br.at[b])
        back_out[b] = yrecv[b]

    UNITS = wg.shape[0]

    def grads_ready():
        ht[...] = jnp.transpose(hb[...])
        dt[pl.ds(0, UNITS), :] = jnp.transpose(dgb[...])
        dt[pl.ds(UNITS, UNITS), :] = jnp.transpose(dub[...])

    def grad_copy(k, i):
        columns = pl.ds(k * WIDE, WIDE)
        slot = k % 2
        src = stage_s.at[slot] if i == 2 else stage_x.at[slot, pl.ds(i * UNITS, UNITS)]
        dst = (gate_out, up_out, down_out)[i]
        return pltpu.make_async_copy(src, dst.at[:, columns], out_sem.at[i, slot])

    def grad_x(k):
        if k > 1:
            grad_copy(k - 2, 0).wait()
            grad_copy(k - 2, 1).wait()
        stage_x[k % 2] = jnp.dot(dt[...], rows_of(xb, k), preferred_element_type=F32).astype(BF16)
        grad_copy(k, 0).start()
        grad_copy(k, 1).start()

    def grad_s(k):
        if k > 1:
            grad_copy(k - 2, 2).wait()
        stage_s[k % 2] = jnp.dot(ht[...], rows_of(sb, k), preferred_element_type=F32).astype(BF16)
        grad_copy(k, 2).start()

    assemble(0)
    first_send(0, 1)
    first_send(0, 0)
    second_send(0, 0, 0)
    second_send(0, 1, 0)
    gate_ready()
    assemble(1)
    first_recv(0, 1)
    first_recv(0, 0)
    second_recv(0, 0, 0)
    second_recv(0, 1, 0)
    first_far(0, 1)
    second_recv(0, 1, 1)
    second_recv(0, 0, 1)
    second_recv(0, 1, 3)
    second_recv(0, 0, 3)
    first_far(0, 0)
    second_far(0, 0, 0)
    second_far(0, 1, 0)
    first_send(1, 0)
    first_send(1, 1)
    second_send(1, 0, 0)
    second_send(1, 1, 0)
    second_far(0, 0, 1)
    second_recv(0, 1, 2)
    second_far(0, 0, 3)
    from_partner(0, 0)
    gate_up(0, 0)
    second_far(0, 1, 1)
    gate_up(0, 1)
    second_recv(0, 0, 2)
    second_far(0, 1, 3)
    from_partner(0, 1)
    gate_up(1, 0)
    first_recv(1, 0)
    first_recv(1, 1)
    from_partner(0, 3)
    gate_up(1, 1)
    second_recv(1, 1, 0)
    second_recv(1, 0, 0)
    gate_up(3, 0)
    second_far(0, 0, 2)
    second_far(0, 1, 2)
    gate_up(3, 1)
    first_far(1, 0)
    second_recv(1, 0, 1)
    second_recv(1, 1, 1)
    from_partner(0, 2)
    gate_up(2, 0)
    second_recv(1, 0, 3)
    gate_up(2, 1)
    first_far(1, 1)
    second_recv(1, 1, 3)
    second_far(1, 1, 0)
    activate(0)
    second_far(1, 0, 0)
    activate(1)
    second_far(1, 1, 1)
    give_ready(0)
    give(0, 2)
    keep(0, 2)
    second_recv(1, 0, 2)
    give(0, 3)
    keep(0, 3)
    second_far(1, 0, 1)
    from_partner(1, 0)
    d_hidden(0, 0)
    second_recv(1, 1, 2)
    second_far(1, 0, 3)
    d_hidden(0, 1)
    second_far(1, 1, 3)
    send_far(0, 0, 2)
    give(0, 1)
    second_far(1, 0, 2)
    keep(0, 1)
    send_far(0, 0, 3)
    give(0, 0)
    keep(0, 0)
    from_partner(1, 1)
    from_partner(1, 3)
    second_far(1, 1, 2)
    give_rest(0)
    d_hidden(1, 0)
    d_hidden(1, 1)
    send_far(0, 0, 1)
    send_mid(0, 0, 2)
    d_hidden(3, 0)
    send_far(0, 0, 0)
    send_mid(0, 0, 3)
    from_partner(1, 2)
    d_hidden(3, 1)
    send_far(0, 1, 2)
    send_far(0, 1, 3)
    d_hidden(2, 0)
    send_far(0, 1, 1)
    send_mid(0, 0, 1)
    send_far(0, 1, 0)
    d_hidden(2, 1)
    activate_back(0)
    activate_back(1)
    give_ready(1)
    give(1, 2)
    send_mid(0, 1, 2)
    finish_first(0, 0, 2)
    send_far2(0, 0)
    send_mid(0, 0, 0)
    send_mid(0, 1, 3)
    send_mid(0, 1, 1)
    keep(1, 2)
    finish_first(0, 0, 3)
    send_far(1, 0, 2)
    send_mid(0, 1, 0)
    give(1, 3)
    finish_first(0, 0, 1)
    keep(1, 3)
    finish_first(0, 1, 2)
    send_far2(0, 1)
    send_mid2(0, 0)
    give(1, 1)
    finish_first(0, 0, 0)
    keep(1, 1)
    finish_first(0, 1, 3)
    send_mid(1, 0, 2)
    send_far(1, 0, 3)
    give(1, 0)
    keep(1, 0)
    finish_first(0, 1, 1)
    send_mid2(0, 1)
    send_far(1, 0, 1)
    give_rest(1)
    grads_ready()
    finish_first(0, 1, 0)
    send_far(1, 0, 0)
    finish_first(1, 0, 2)
    send_far2(1, 0)
    grad_x(0)
    send_far(1, 1, 2)
    send_mid(1, 0, 3)
    send_far(1, 1, 3)
    send_far(1, 1, 1)
    send_back(0)
    send_far(1, 1, 0)
    grad_s(0)
    send_mid(1, 0, 1)
    grad_x(1)
    send_mid(1, 1, 2)
    send_mid(1, 0, 0)
    send_mid(1, 1, 3)
    finish_first(1, 0, 3)
    grad_s(1)
    send_mid(1, 1, 1)
    back_here(0)
    grad_x(2)
    finish_first(1, 0, 1)
    send_mid(1, 1, 0)
    send_mid2(1, 0)
    grad_s(2)
    finish_first(1, 1, 2)
    send_far2(1, 1)
    finish_first(1, 0, 0)
    grad_x(3)
    finish_first(1, 1, 3)
    grad_s(3)
    grad_x(4)
    grad_s(4)
    finish_first(1, 1, 1)
    send_mid2(1, 1)
    grad_x(5)
    finish_first(1, 1, 0)
    grad_s(5)
    grad_x(6)
    grad_s(6)
    grad_x(7)
    send_back(1)
    grad_s(7)
    back_here(1)

    for k in (ETS - 2, ETS - 1):
        for i in range(3):
            grad_copy(k, i).wait()
    wait_bytes(psend, qs)
    for a in (0, 1):
        wait_bytes(pack.at[a, three], ys.at[a])
        wait_bytes(ysend.at[a, three], bs.at[a])
        wait_bytes(bufs[a].at[:, pl.ds(0, ETS)], ps.at[a])
        thirty = bufs[a].at[pl.ds(0, 2), pl.ds(0, 15)]
        wait_bytes(thirty, ring_s.at[a])
        wait_bytes(thirty, sum_s.at[a])


def spread_back(routes, probs, back, layer_out, token_out):
    count = layer_out.shape[0]
    square = (count, count)
    route = routes[...].astype(F32)
    prob = probs[...]
    r0 = jnp.transpose(jnp.broadcast_to(route[0:1], square))
    r1 = jnp.transpose(jnp.broadcast_to(route[1:2], square))
    p0 = jnp.transpose(jnp.broadcast_to(prob[0:1], square))[:, 0:1]
    p1 = jnp.transpose(jnp.broadcast_to(prob[1:2], square))[:, 0:1]
    first = lax.broadcasted_iota(jnp.int32, square, 0)
    second = lax.broadcasted_iota(jnp.int32, square, 1)
    before = jnp.where(second < first, 1.0, 0.0).astype(BF16)
    lane = second.astype(F32)
    layer = [jnp.zeros((count, PART), F32) for _ in FLOWS]
    token = [jnp.zeros((count, PART), F32) for _ in FLOWS]
    for e in range(EXP):
        in0 = jnp.where(r0 == e, 1.0, 0.0)
        in1 = jnp.where(r1 == e, 1.0, 0.0)
        member = in0 + in1
        placed = jnp.dot(before, member.astype(BF16), preferred_element_type=F32)
        weight = in0[:, 0:1] * p0 + in1[:, 0:1] * p1
        for h in FLOWS:
            pick = jnp.where(placed + h * CAP == lane, member, 0.0)
            pick = jnp.where((lane >= h * CAP) & (lane < (h + 1) * CAP), pick, 0.0)
            pick = pick[:, :2 * CAP].astype(BF16)
            layer[h] = layer[h] + weight * jnp.dot(pick, back[0, e], preferred_element_type=F32)
            token[h] = token[h] + jnp.dot(pick, back[1, e], preferred_element_type=F32)
    layer_out[...] = jnp.concatenate(layer, axis=1).astype(BF16)
    token_out[...] = jnp.concatenate(token, axis=1).astype(BF16)


def finish_kernel(routes, probs, back, gate_in, up_in, down_in, layer_out, token_out, gate_out, up_out, down_out, held, sem):
    pairs = ((gate_in, gate_out), (up_in, up_out), (down_in, down_out))
    blocks = 4
    rows = gate_in.shape[0] // blocks

    def move(i, k, way):
        part = pl.ds(k * rows, rows)
        src, dst = pairs[i]
        if way == 0:
            return pltpu.make_async_copy(src.at[part], held.at[i, part], sem.at[0, i, k])
        return pltpu.make_async_copy(held.at[i, part], dst.at[part], sem.at[1, i, k])

    steps = [(i, k) for i in range(3) for k in range(blocks)]
    for i, k in steps:
        move(i, k, 0).start()
    for i, k in steps:
        move(i, k, 0).wait()
        move(i, k, 1).start()
    spread_back(routes, probs, back, layer_out, token_out)
    for i, k in steps:
        move(i, k, 1).wait()


def per_device(tokens, routes, route_probs, grad_out, w_gate, w_up, w_down):
    units, width = w_gate.shape
    count = tokens.shape[0]
    vmem = pl.BlockSpec(memory_space=pltpu.VMEM)
    anywhere = pl.BlockSpec(memory_space=pl.ANY)
    dma = pltpu.SemaphoreType.DMA
    back_shape = jax.ShapeDtypeStruct((2, EXP, 2 * CAP, PART), BF16)
    weight_buf = pltpu.VMEM((ETS, units, WIDE), BF16)
    gather_buf = pltpu.VMEM((SIDE, 2 * ETS, ROWS, PART), BF16)
    acc = pltpu.VMEM((ALL_ROWS, units), F32)
    hidden_buf = pltpu.VMEM((ALL_ROWS, units), BF16)
    packed = pltpu.VMEM((2, EXP, 2 * CAP, PART), BF16)
    routes_t = routes.T
    probs_t = route_probs.T
    grad_shape = jax.ShapeDtypeStruct((units, width), BF16)
    gate, up, down, back = pl.pallas_call(
        main_kernel,
        out_shape=(grad_shape, grad_shape, grad_shape, back_shape),
        in_specs=[vmem] * 4 + [anywhere] * 3,
        out_specs=(anywhere, anywhere, anywhere, vmem),
        scratch_shapes=[
            packed, packed, gather_buf, gather_buf, weight_buf, weight_buf, weight_buf,
            acc, acc, acc, hidden_buf, hidden_buf, hidden_buf,
            pltpu.VMEM((2, 2, SIDE, SIDE, ROWS, PART), F32),
            pltpu.VMEM((2, SIDE, SIDE, ROWS, PART), BF16),
            pltpu.VMEM((2, 2, SIDE, SIDE, ROWS, PART), BF16),
            pltpu.VMEM((2, 2, SIDE, ROWS, PART), BF16),
            pltpu.VMEM((2, 2, SIDE, 2, HALF, PART), BF16),
            pltpu.VMEM((2, 2, SIDE, 2, ROWS, PART), BF16),
            pltpu.VMEM((2, 2, SIDE, 2, ROWS, PART), BF16),
            pltpu.VMEM((2, 2, ROWS, PART), BF16),
            pltpu.VMEM((2, 2, 2, HALF, PART), BF16),
            pltpu.VMEM((2, 2, 2, ROWS, PART), BF16),
            pltpu.VMEM((2, 2, 2, ROWS, PART), BF16),
            packed, packed,
            pltpu.VMEM((units, ALL_ROWS), BF16),
            pltpu.VMEM((2 * units, ALL_ROWS), BF16),
            pltpu.VMEM((2, 2 * units, WIDE), BF16),
            pltpu.VMEM((2, units, WIDE), BF16),
            dma((3,)), dma((3, 2)), dma((2,)), dma((2,)),
            dma((2, 2)), dma((2, 2)), dma((2, 2, 4)), dma((2, 2, 4)), dma((2,)), dma((2,)), dma((2, 4)),
            dma(()), dma((2, 2, 4)), dma((2, 2, 4)), dma((2, 2, 4)), dma((2, 2)), dma((2, 2)), dma((2,)),
            dma((2,)), dma((2,)),
        ],
        compiler_params=pltpu.CompilerParams(collective_id=0, has_side_effects=True, vmem_limit_bytes=VMEM_LIMIT),
        name="expert_layer",
    )(routes_t, probs_t, tokens, grad_out, w_gate, w_up, w_down)

    token_shape = jax.ShapeDtypeStruct(tokens.shape, BF16)
    return pl.pallas_call(
        finish_kernel,
        out_shape=(token_shape, token_shape, grad_shape, grad_shape, grad_shape),
        in_specs=[vmem] * 3 + [anywhere] * 3,
        out_specs=(vmem, vmem, anywhere, anywhere, anywhere),
        scratch_shapes=[pltpu.VMEM((3, units, width), BF16), dma((2, 3, 4))],
        compiler_params=pltpu.CompilerParams(vmem_limit_bytes=VMEM_LIMIT),
        name="finish",
    )(routes_t, probs_t, back, gate, up, down)


def solution(mesh):
    return jax.shard_map(
        per_device,
        mesh=mesh,
        in_specs=(
            P("dp", "et"),
            P("dp", None),
            P("dp", None),
            P("dp", "et"),
            P(("dp", "et"), None),
            P(("dp", "et"), None),
            P(("dp", "et"), None),
        ),
        out_specs=(
            P("dp", "et"),
            P("dp", "et"),
            P(("dp", "et"), None),
            P(("dp", "et"), None),
            P(("dp", "et"), None),
        ),
        check_vma=False,
    )
```

```python
import jax
import jax.numpy as jnp
from jax import lax
from jax.experimental import pallas as pl
from jax.experimental.pallas import tpu as pltpu
from jax.sharding import PartitionSpec as P

MESH = pl.DeviceIdType.MESH
EXP = 4
CAP = 40
SIDE = 4
ROWS = SIDE * CAP
ALL_ROWS = SIDE * ROWS
HALF = ROWS // 2
ETS = 8
WIDE = 512
PART = 256
F32 = jnp.float32
BF16 = jnp.bfloat16
NT = (((1,), (1,)), ((), ()))
FLOWS = (0, 1)
VMEM_LIMIT = 62 * 1024 * 1024


def place():
    dp = lax.axis_index("dp")
    et = lax.axis_index("et")
    return lax.div(dp, SIDE), lax.rem(dp, SIDE), lax.div(et, 2), lax.rem(et, 2)


def turn(value, by):
    return lax.rem(value + by, SIDE)


def device(y, z, x, c):
    return (y * SIDE + z, x * 2 + c)


def remote(src, dst, send_sem, recv_sem, target):
    return pltpu.make_async_remote_copy(
        src_ref=src, dst_ref=dst, send_sem=send_sem, recv_sem=recv_sem, device_id=target, device_id_type=MESH
    )


def greet(y, z, x, c):
    barrier = pltpu.get_barrier_semaphore()
    others = [device(y, z, x, 1 - c)]
    others += [device(y, z, turn(x, 1), c), device(y, z, turn(x, 3), c)]
    others += [device(y, turn(z, 1), x, c), device(y, turn(z, 3), x, c)]
    others += [device(turn(y, by), z, x, c) for by in (1, 2, 3)]
    for other in others:
        pl.semaphore_signal(barrier, inc=1, device_id=other, device_id_type=MESH)
    return lambda: pl.semaphore_wait(barrier, len(others))


def halves_below(value):
    return jnp.concatenate([value[:, :PART], value[:, PART:]], axis=0)


def pack_rows(routes, probs, tok, cot, pack):
    count = tok.shape[0]
    slots = (CAP, count)
    route = routes[...].astype(F32)
    prob = probs[...]
    r0 = jnp.broadcast_to(route[0:1], slots)
    r1 = jnp.broadcast_to(route[1:2], slots)
    p0 = jnp.broadcast_to(prob[0:1], slots)
    p1 = jnp.broadcast_to(prob[1:2], slots)
    square = (count, count)
    first = lax.broadcasted_iota(jnp.int32, square, 0)
    second = lax.broadcasted_iota(jnp.int32, square, 1)
    before = jnp.where(first < second, 1.0, 0.0).astype(BF16)
    slot = lax.broadcasted_iota(jnp.int32, slots, 0).astype(F32)
    x_all = tok[...]
    d_all = cot[...]
    for e in range(EXP):
        in0 = jnp.where(r0 == e, 1.0, 0.0)
        in1 = jnp.where(r1 == e, 1.0, 0.0)
        member = in0 + in1
        placed = jnp.dot(member.astype(BF16), before, preferred_element_type=F32)
        pick = jnp.where(placed == slot, member, 0.0)
        weight = jnp.sum(pick * (in0 * p0 + in1 * p1), axis=1, keepdims=True)
        pick = pick.astype(BF16)
        chosen = jnp.dot(pick, x_all, preferred_element_type=F32)
        scaled = weight * jnp.dot(pick, d_all, preferred_element_type=F32)
        pack[0, e] = halves_below(chosen).astype(BF16)
        pack[1, e] = halves_below(scaled).astype(BF16)


def main_kernel(
    routes, probs, tok, cot, wg, wu, wd, gate_out, up_out, down_out, back_out,
    pack, recv, xb, sb, wgv, wuv, wdv, acc_g, acc_u, acc_d, hb, dgb, dub,
    own, psend, precv, far, farr, mid, midr, far2, far2r, mid2, mid2r, ysend, yrecv, ht, dt, stage_x, stage_s,
    w_sem, out_sem, ys, yr, n1r, h1r, n2r, h2r, ring_s, ps, pr, qs, qr, fr, mr, f2r, m2r, sum_s, bs, br,
):
    y, z, x, c = place()
    weights = ((wg, wgv), (wu, wuv), (wd, wdv))
    for i, (src, dst) in enumerate(weights):
        for k in range(ETS):
            pltpu.make_async_copy(src.at[:, pl.ds(k * WIDE, WIDE)], dst.at[k], w_sem.at[i]).start()

    def wait_bytes(ref, sem):
        pltpu.make_async_copy(ref, ref, sem).wait()

    await_greetings = greet(y, z, x, c)
    pack_rows(routes, probs, tok, cot, pack)
    await_greetings()

    for a in (0, 1):
        for by in (1, 2, 3):
            e = turn(y, by)
            remote(pack.at[a, e], recv.at[a, y], ys.at[a], yr.at[a], device(e, z, x, c)).start()

    bufs = (xb, sb)
    own_et = x * 2 + c
    partner = device(y, z, x, 1 - c)
    low, high = pl.ds(0, HALF), pl.ds(HALF, HALF)
    three = pl.ds(0, 3)

    def assemble(a):
        recv[a, y] = pack[a, y]
        wait_bytes(recv.at[a, three], yr.at[a])
        parts = [recv[a, i].astype(F32) for i in range(SIDE)]
        for h in FLOWS:
            piece = [part[h * CAP:(h + 1) * CAP] for part in parts]
            bufs[a][z, own_et * 2 + h] = jnp.concatenate(piece, axis=0).astype(BF16)

    def chunk(a, h, first, second):
        if h == 0:
            return bufs[a].at[second, (first * 2 + c) * 2]
        return bufs[a].at[first, (second * 2 + c) * 2 + 1]

    def mine(h):
        return (x, z) if h == 0 else (z, x)

    def on_x(by):
        return device(y, z, turn(x, by), c)

    def on_z(by):
        return device(y, turn(z, by), x, c)

    def first_dev(h, by):
        return on_x(by) if h == 0 else on_z(by)

    def second_dev(h, by):
        return on_z(by) if h == 0 else on_x(by)

    GO = (1, 3)
    COME = (3, 1)
    one_chunk = xb.at[0, 0]
    two_chunks = xb.at[0, pl.ds(0, 2)]

    def to_partner(a, h, i, j):
        f, s = mine(h)
        ref = chunk(a, h, turn(f, j), turn(s, i))
        remote(ref, ref, ps.at[a], pr.at[a, j if h == 0 else i], partner).start()

    def from_partner(a, group):
        wait_bytes(bufs[a].at[0, pl.ds(0, ETS)], pr.at[a, group])

    def first_send(a, h):
        f, s = mine(h)
        ref = chunk(a, h, f, s)
        for d in (0, 1):
            remote(ref, ref, ring_s.at[a], n1r.at[a, h], first_dev(h, GO[d])).start()

    def second_send(a, h, j):
        f, s = mine(h)
        ref = chunk(a, h, turn(f, j), s)
        for d in (0, 1):
            remote(ref, ref, ring_s.at[a], n2r.at[a, h, j], second_dev(h, GO[d])).start()
        to_partner(a, h, 0, j)

    def first_recv(a, h):
        f, s = mine(h)
        wait_bytes(two_chunks, n1r.at[a, h])
        for d in (0, 1):
            ref = chunk(a, h, turn(f, COME[d]), s).at[low if d == 0 else high]
            remote(ref, ref, ring_s.at[a], h1r.at[a, h], first_dev(h, GO[d])).start()
        second_send(a, h, 1)
        second_send(a, h, 3)

    def first_far(a, h):
        wait_bytes(one_chunk, h1r.at[a, h])
        second_send(a, h, 2)

    def second_recv(a, h, j):
        f, s = mine(h)
        wait_bytes(two_chunks, n2r.at[a, h, j])
        for d in (0, 1):
            ref = chunk(a, h, turn(f, j), turn(s, COME[d])).at[low if d == 0 else high]
            remote(ref, ref, ring_s.at[a], h2r.at[a, h, j], second_dev(h, GO[d])).start()
        for d in (0, 1):
            to_partner(a, h, COME[d], j)

    def second_far(a, h, j):
        wait_bytes(one_chunk, h2r.at[a, h, j])
        to_partner(a, h, 2, j)

    def rows_of(buf, k):
        left = buf[:, k * 2].reshape(ALL_ROWS, PART)
        right = buf[:, k * 2 + 1].reshape(ALL_ROWS, PART)
        return jnp.concatenate([left, right], axis=1)

    def gate_ready():
        wait_bytes(wgv, w_sem.at[0])
        wait_bytes(wuv, w_sem.at[1])
        wait_bytes(wdv, w_sem.at[2])

    def add_to(acc, value, first):
        if first:
            acc[...] = value
        else:
            acc[...] += value

    def gate_up(group, core):
        k = turn(x, group) * 2 + core
        first = group == 0 and core == 0
        rows = rows_of(xb, k)
        add_to(acc_g, lax.dot_general(rows, wgv[k], NT, preferred_element_type=F32), first)
        add_to(acc_u, lax.dot_general(rows, wuv[k], NT, preferred_element_type=F32), first)

    def d_hidden(group, core):
        k = turn(x, group) * 2 + core
        first = group == 0 and core == 0
        add_to(acc_d, lax.dot_general(rows_of(sb, k), wdv[k], NT, preferred_element_type=F32), first)

    STEPS = ALL_ROWS // 64

    def activate(part):
        def step(i, carry):
            rows = pl.ds(pl.multiple_of(i * 32, 32), 32)
            gate = acc_g[rows, :]
            up = acc_u[rows, :]
            squash = jax.nn.sigmoid(gate)
            active = gate * squash
            hb[rows, :] = (active * up).astype(BF16)
            acc_g[rows, :] = up * squash * (1.0 + gate * (1.0 - squash))
            acc_u[rows, :] = active
            return carry

        lax.fori_loop(part * STEPS, (part + 1) * STEPS, step, 0)

    def activate_back(part):
        def step(i, carry):
            rows = pl.ds(pl.multiple_of(i * 32, 32), 32)
            back = acc_d[rows, :]
            dgb[rows, :] = (back * acc_g[rows, :]).astype(BF16)
            dub[rows, :] = (back * acc_u[rows, :]).astype(BF16)
            return carry

        lax.fori_loop(part * STEPS, (part + 1) * STEPS, step, 0)

    stacked = (SIDE, ROWS, PART)

    def give_ready(b):
        if b == 1:
            wait_bytes(psend, qs)

    def pair_here(b, j):
        wait_bytes(precv.at[b, turn(x, j)], qr.at[b, j])

    def product(b, et):
        if b == 0:
            return jnp.dot(hb[...], wdv[et], preferred_element_type=F32)
        out = jnp.dot(dgb[...], wgv[et], preferred_element_type=F32)
        return out + jnp.dot(dub[...], wuv[et], preferred_element_type=F32)

    def give(b, j):
        at = turn(x, j)
        other = product(b, at * 2 + 1 - c).astype(BF16)
        psend[at, 0] = other[:, :PART].reshape(stacked)
        psend[at, 1] = other[:, PART:].reshape(stacked)
        remote(psend.at[at], precv.at[b, at], qs, qr.at[b, j], partner).start()

    def keep(b, j):
        at = turn(x, j)
        value = product(b, at * 2 + c)
        own[b, at, 0] = value[:, :PART].reshape(stacked)
        own[b, at, 1] = value[:, PART:].reshape(stacked)

    def ring1(h, by):
        return on_z(by) if h == 0 else on_x(by)

    def ring2(h, by):
        return on_x(by) if h == 0 else on_z(by)

    def spot(h, j, by):
        return (turn(x, j), turn(z, by)) if h == 0 else (turn(x, by), turn(z, j))

    def pair_sum(b, h, j, by):
        xx, zz = spot(h, j, by)
        return own[b, xx, h, zz] + precv[b, xx, h, zz].astype(F32)

    def send_far(b, h, j):
        far[b, h, j] = pair_sum(b, h, j, 2).astype(BF16)
        for d, part in ((0, high), (1, low)):
            remote(far.at[b, h, j, part], farr.at[b, h, j, d], sum_s.at[b], fr.at[b, h, j], ring1(h, GO[d])).start()

    def add_half(total, part, d):
        if d == 0:
            return jnp.concatenate([total[:HALF], total[HALF:] + part], axis=0)
        return jnp.concatenate([total[:HALF] + part, total[HALF:]], axis=0)

    def send_mid(b, h, j):
        wait_bytes(farr.at[b, h, j], fr.at[b, h, j])
        for d in (0, 1):
            total = add_half(pair_sum(b, h, j, GO[d]), farr[b, h, j, d].astype(F32), d)
            mid[b, h, j, d] = total.astype(BF16)
            remote(mid.at[b, h, j, d], midr.at[b, h, j, d], sum_s.at[b], mr.at[b, h, j], ring1(h, GO[d])).start()

    def finish_first(b, h, j):
        wait_bytes(midr.at[b, h, j], mr.at[b, h, j])
        xx, zz = spot(h, j, 0)
        total = pair_sum(b, h, j, 0)
        own[b, xx, h, zz] = total + midr[b, h, j, 0].astype(F32) + midr[b, h, j, 1].astype(F32)

    def first_sum(b, h, j):
        xx, zz = spot(h, j, 0)
        return own[b, xx, h, zz]

    def send_far2(b, h):
        far2[b, h] = first_sum(b, h, 2).astype(BF16)
        for d, part in ((0, high), (1, low)):
            remote(far2.at[b, h, part], far2r.at[b, h, d], sum_s.at[b], f2r.at[b, h], ring2(h, GO[d])).start()

    def send_mid2(b, h):
        wait_bytes(far2r.at[b, h], f2r.at[b, h])
        for d in (0, 1):
            total = add_half(first_sum(b, h, GO[d]), far2r[b, h, d].astype(F32), d)
            mid2[b, h, d] = total.astype(BF16)
            remote(mid2.at[b, h, d], mid2r.at[b, h, d], sum_s.at[b], m2r.at[b, h], ring2(h, GO[d])).start()

    def send_back(b):
        totals = []
        for h in FLOWS:
            wait_bytes(mid2r.at[b, h], m2r.at[b, h])
            total = first_sum(b, h, 0) + mid2r[b, h, 0].astype(F32) + mid2r[b, h, 1].astype(F32)
            totals.append(total)
        for i in range(SIDE):
            piece = [total[i * CAP:(i + 1) * CAP] for total in totals]
            ysend[b, i] = jnp.concatenate(piece, axis=0).astype(BF16)
        for by in (1, 2, 3):
            target = turn(y, by)
            remote(ysend.at[b, target], yrecv.at[b, y], bs.at[b], br.at[b], device(target, z, x, c)).start()
        yrecv[b, y] = ysend[b, y]

    def back_here(b):
        wait_bytes(yrecv.at[b, three], br.at[b])
        back_out[b] = yrecv[b]

    UNITS = wg.shape[0]

    def grads_ready():
        ht[...] = jnp.transpose(hb[...])
        dt[pl.ds(0, UNITS), :] = jnp.transpose(dgb[...])
        dt[pl.ds(UNITS, UNITS), :] = jnp.transpose(dub[...])

    def grad_copy(k, i):
        columns = pl.ds(k * WIDE, WIDE)
        slot = k % 2
        src = stage_s.at[slot] if i == 2 else stage_x.at[slot, pl.ds(i * UNITS, UNITS)]
        dst = (gate_out, up_out, down_out)[i]
        return pltpu.make_async_copy(src, dst.at[:, columns], out_sem.at[i, slot])

    def grad_x(k):
        if k > 1:
            grad_copy(k - 2, 0).wait()
            grad_copy(k - 2, 1).wait()
        stage_x[k % 2] = jnp.dot(dt[...], rows_of(xb, k), preferred_element_type=F32).astype(BF16)
        grad_copy(k, 0).start()
        grad_copy(k, 1).start()

    def grad_s(k):
        if k > 1:
            grad_copy(k - 2, 2).wait()
        stage_s[k % 2] = jnp.dot(ht[...], rows_of(sb, k), preferred_element_type=F32).astype(BF16)
        grad_copy(k, 2).start()

    assemble(0)
    first_send(0, 1)
    first_send(0, 0)
    second_send(0, 0, 0)
    second_send(0, 1, 0)
    gate_ready()
    assemble(1)
    first_recv(0, 1)
    first_recv(0, 0)
    second_recv(0, 0, 0)
    second_recv(0, 1, 0)
    first_far(0, 1)
    second_recv(0, 1, 1)
    second_recv(0, 0, 1)
    second_recv(0, 1, 3)
    second_recv(0, 0, 3)
    first_far(0, 0)
    second_far(0, 0, 0)
    second_far(0, 1, 0)
    first_send(1, 1)
    first_send(1, 0)
    second_send(1, 0, 0)
    second_send(1, 1, 0)
    second_far(0, 0, 1)
    second_recv(0, 1, 2)
    second_far(0, 0, 3)
    from_partner(0, 0)
    gate_up(0, 0)
    second_far(0, 1, 1)
    gate_up(0, 1)
    second_far(0, 1, 3)
    second_recv(0, 0, 2)
    from_partner(0, 1)
    gate_up(1, 0)
    first_recv(1, 0)
    first_recv(1, 1)
    from_partner(0, 3)
    gate_up(1, 1)
    second_recv(1, 1, 0)
    second_recv(1, 0, 0)
    gate_up(3, 0)
    second_far(0, 0, 2)
    second_far(0, 1, 2)
    gate_up(3, 1)
    first_far(1, 0)
    second_recv(1, 0, 1)
    second_recv(1, 1, 1)
    from_partner(0, 2)
    gate_up(2, 0)
    second_recv(1, 0, 3)
    gate_up(2, 1)
    first_far(1, 1)
    second_recv(1, 1, 3)
    second_far(1, 1, 0)
    activate(0)
    second_far(1, 0, 0)
    activate(1)
    second_far(1, 1, 1)
    give_ready(0)
    give(0, 2)
    keep(0, 2)
    second_recv(1, 0, 2)
    give(0, 3)
    keep(0, 3)
    second_far(1, 0, 1)
    from_partner(1, 0)
    d_hidden(0, 0)
    second_recv(1, 1, 2)
    second_far(1, 0, 3)
    give(0, 1)
    second_far(1, 1, 3)
    keep(0, 1)
    pair_here(0, 2)
    send_far(0, 1, 3)
    send_far(0, 1, 1)
    second_far(1, 0, 2)
    send_far(0, 0, 2)
    send_far(0, 1, 2)
    send_far(0, 1, 0)
    give(0, 0)
    pair_here(0, 3)
    send_far(0, 0, 3)
    second_far(1, 1, 2)
    keep(0, 0)
    d_hidden(0, 1)
    from_partner(1, 1)
    from_partner(1, 3)
    d_hidden(1, 0)
    d_hidden(1, 1)
    d_hidden(3, 0)
    send_mid(0, 0, 2)
    pair_here(0, 1)
    send_mid(0, 1, 3)
    send_far(0, 0, 1)
    send_mid(0, 1, 2)
    send_mid(0, 0, 3)
    pair_here(0, 0)
    send_mid(0, 1, 1)
    send_mid(0, 1, 0)
    send_far(0, 0, 0)
    from_partner(1, 2)
    d_hidden(3, 1)
    d_hidden(2, 0)
    d_hidden(2, 1)
    activate_back(0)
    activate_back(1)
    finish_first(0, 0, 2)
    send_far2(0, 0)
    finish_first(0, 1, 3)
    give_ready(1)
    give(1, 2)
    send_mid(0, 0, 1)
    keep(1, 2)
    finish_first(0, 1, 2)
    send_far2(0, 1)
    finish_first(0, 0, 3)
    give(1, 3)
    send_mid(0, 0, 0)
    finish_first(0, 1, 1)
    keep(1, 3)
    pair_here(1, 2)
    send_far(1, 0, 2)
    send_far(1, 1, 2)
    send_far(1, 1, 3)
    finish_first(0, 1, 0)
    send_far(1, 1, 0)
    send_far(1, 1, 1)
    finish_first(0, 0, 1)
    give(1, 1)
    pair_here(1, 3)
    send_far(1, 0, 3)
    send_mid2(0, 1)
    send_mid2(0, 0)
    keep(1, 1)
    finish_first(0, 0, 0)
    give(1, 0)
    send_mid(1, 0, 2)
    keep(1, 0)
    pair_here(1, 1)
    send_mid(1, 1, 2)
    send_mid(1, 1, 0)
    send_mid(1, 1, 3)
    send_far(1, 0, 1)
    send_mid(1, 1, 1)
    send_mid(1, 0, 3)
    grads_ready()
    send_back(0)
    pair_here(1, 0)
    send_far(1, 0, 0)
    finish_first(1, 0, 2)
    send_far2(1, 0)
    grad_x(0)
    send_mid(1, 0, 1)
    finish_first(1, 1, 2)
    send_far2(1, 1)
    grad_s(0)
    finish_first(1, 1, 0)
    finish_first(1, 0, 3)
    grad_x(1)
    back_here(0)
    send_mid(1, 0, 0)
    finish_first(1, 1, 3)
    grad_s(1)
    grad_x(2)
    finish_first(1, 0, 1)
    finish_first(1, 1, 1)
    grad_s(2)
    send_mid2(1, 1)
    send_mid2(1, 0)
    grad_x(3)
    finish_first(1, 0, 0)
    grad_s(3)
    grad_x(4)
    grad_s(4)
    grad_x(5)
    send_back(1)
    grad_s(5)
    grad_x(6)
    grad_s(6)
    grad_x(7)
    grad_s(7)
    back_here(1)

    for k in (ETS - 2, ETS - 1):
        for i in range(3):
            grad_copy(k, i).wait()
    wait_bytes(psend, qs)
    for a in (0, 1):
        wait_bytes(pack.at[a, three], ys.at[a])
        wait_bytes(ysend.at[a, three], bs.at[a])
        wait_bytes(bufs[a].at[:, pl.ds(0, ETS)], ps.at[a])
        thirty = bufs[a].at[pl.ds(0, 2), pl.ds(0, 15)]
        wait_bytes(thirty, ring_s.at[a])
        wait_bytes(thirty, sum_s.at[a])


def spread_back(routes, probs, back, layer_out, token_out):
    count = layer_out.shape[0]
    square = (count, count)
    route = routes[...].astype(F32)
    prob = probs[...]
    r0 = jnp.transpose(jnp.broadcast_to(route[0:1], square))
    r1 = jnp.transpose(jnp.broadcast_to(route[1:2], square))
    p0 = jnp.transpose(jnp.broadcast_to(prob[0:1], square))[:, 0:1]
    p1 = jnp.transpose(jnp.broadcast_to(prob[1:2], square))[:, 0:1]
    first = lax.broadcasted_iota(jnp.int32, square, 0)
    second = lax.broadcasted_iota(jnp.int32, square, 1)
    before = jnp.where(second < first, 1.0, 0.0).astype(BF16)
    lane = second.astype(F32)
    layer = [jnp.zeros((count, PART), F32) for _ in FLOWS]
    token = [jnp.zeros((count, PART), F32) for _ in FLOWS]
    for e in range(EXP):
        in0 = jnp.where(r0 == e, 1.0, 0.0)
        in1 = jnp.where(r1 == e, 1.0, 0.0)
        member = in0 + in1
        placed = jnp.dot(before, member.astype(BF16), preferred_element_type=F32)
        weight = in0[:, 0:1] * p0 + in1[:, 0:1] * p1
        for h in FLOWS:
            pick = jnp.where(placed + h * CAP == lane, member, 0.0)
            pick = jnp.where((lane >= h * CAP) & (lane < (h + 1) * CAP), pick, 0.0)
            pick = pick[:, :2 * CAP].astype(BF16)
            layer[h] = layer[h] + weight * jnp.dot(pick, back[0, e], preferred_element_type=F32)
            token[h] = token[h] + jnp.dot(pick, back[1, e], preferred_element_type=F32)
    layer_out[...] = jnp.concatenate(layer, axis=1).astype(BF16)
    token_out[...] = jnp.concatenate(token, axis=1).astype(BF16)


def finish_kernel(routes, probs, back, gate_in, up_in, down_in, layer_out, token_out, gate_out, up_out, down_out, held, sem):
    pairs = ((gate_in, gate_out), (up_in, up_out), (down_in, down_out))
    blocks = 4
    rows = gate_in.shape[0] // blocks

    def move(i, k, way):
        part = pl.ds(k * rows, rows)
        src, dst = pairs[i]
        if way == 0:
            return pltpu.make_async_copy(src.at[part], held.at[i, part], sem.at[0, i, k])
        return pltpu.make_async_copy(held.at[i, part], dst.at[part], sem.at[1, i, k])

    steps = [(i, k) for i in range(3) for k in range(blocks)]
    for i, k in steps:
        move(i, k, 0).start()
    for i, k in steps:
        move(i, k, 0).wait()
        move(i, k, 1).start()
    spread_back(routes, probs, back, layer_out, token_out)
    for i, k in steps:
        move(i, k, 1).wait()


def per_device(tokens, routes, route_probs, grad_out, w_gate, w_up, w_down):
    units, width = w_gate.shape
    count = tokens.shape[0]
    vmem = pl.BlockSpec(memory_space=pltpu.VMEM)
    anywhere = pl.BlockSpec(memory_space=pl.ANY)
    dma = pltpu.SemaphoreType.DMA
    back_shape = jax.ShapeDtypeStruct((2, EXP, 2 * CAP, PART), BF16)
    weight_buf = pltpu.VMEM((ETS, units, WIDE), BF16)
    gather_buf = pltpu.VMEM((SIDE, 2 * ETS, ROWS, PART), BF16)
    acc = pltpu.VMEM((ALL_ROWS, units), F32)
    hidden_buf = pltpu.VMEM((ALL_ROWS, units), BF16)
    packed = pltpu.VMEM((2, EXP, 2 * CAP, PART), BF16)
    routes_t = routes.T
    probs_t = route_probs.T
    grad_shape = jax.ShapeDtypeStruct((units, width), BF16)
    gate, up, down, back = pl.pallas_call(
        main_kernel,
        out_shape=(grad_shape, grad_shape, grad_shape, back_shape),
        in_specs=[vmem] * 4 + [anywhere] * 3,
        out_specs=(anywhere, anywhere, anywhere, vmem),
        scratch_shapes=[
            packed, packed, gather_buf, gather_buf, weight_buf, weight_buf, weight_buf,
            acc, acc, acc, hidden_buf, hidden_buf, hidden_buf,
            pltpu.VMEM((2, SIDE, 2, SIDE, ROWS, PART), F32),
            pltpu.VMEM((SIDE, 2, SIDE, ROWS, PART), BF16),
            pltpu.VMEM((2, SIDE, 2, SIDE, ROWS, PART), BF16),
            pltpu.VMEM((2, 2, SIDE, ROWS, PART), BF16),
            pltpu.VMEM((2, 2, SIDE, 2, HALF, PART), BF16),
            pltpu.VMEM((2, 2, SIDE, 2, ROWS, PART), BF16),
            pltpu.VMEM((2, 2, SIDE, 2, ROWS, PART), BF16),
            pltpu.VMEM((2, 2, ROWS, PART), BF16),
            pltpu.VMEM((2, 2, 2, HALF, PART), BF16),
            pltpu.VMEM((2, 2, 2, ROWS, PART), BF16),
            pltpu.VMEM((2, 2, 2, ROWS, PART), BF16),
            packed, packed,
            pltpu.VMEM((units, ALL_ROWS), BF16),
            pltpu.VMEM((2 * units, ALL_ROWS), BF16),
            pltpu.VMEM((2, 2 * units, WIDE), BF16),
            pltpu.VMEM((2, units, WIDE), BF16),
            dma((3,)), dma((3, 2)), dma((2,)), dma((2,)),
            dma((2, 2)), dma((2, 2)), dma((2, 2, 4)), dma((2, 2, 4)), dma((2,)), dma((2,)), dma((2, 4)),
            dma(()), dma((2, 4)), dma((2, 2, 4)), dma((2, 2, 4)), dma((2, 2)), dma((2, 2)), dma((2,)),
            dma((2,)), dma((2,)),
        ],
        compiler_params=pltpu.CompilerParams(collective_id=0, has_side_effects=True, vmem_limit_bytes=VMEM_LIMIT),
        name="expert_layer",
    )(routes_t, probs_t, tokens, grad_out, w_gate, w_up, w_down)

    token_shape = jax.ShapeDtypeStruct(tokens.shape, BF16)
    return pl.pallas_call(
        finish_kernel,
        out_shape=(token_shape, token_shape, grad_shape, grad_shape, grad_shape),
        in_specs=[vmem] * 3 + [anywhere] * 3,
        out_specs=(vmem, vmem, anywhere, anywhere, anywhere),
        scratch_shapes=[pltpu.VMEM((3, units, width), BF16), dma((2, 3, 4))],
        compiler_params=pltpu.CompilerParams(vmem_limit_bytes=VMEM_LIMIT),
        name="finish",
    )(routes_t, probs_t, back, gate, up, down)


def solution(mesh):
    return jax.shard_map(
        per_device,
        mesh=mesh,
        in_specs=(
            P("dp", "et"),
            P("dp", None),
            P("dp", None),
            P("dp", "et"),
            P(("dp", "et"), None),
            P(("dp", "et"), None),
            P(("dp", "et"), None),
        ),
        out_specs=(
            P("dp", "et"),
            P("dp", "et"),
            P(("dp", "et"), None),
            P(("dp", "et"), None),
            P(("dp", "et"), None),
        ),
        check_vma=False,
    )
```

```python
import jax
import jax.numpy as jnp
from jax import lax
from jax.experimental import pallas as pl
from jax.experimental.pallas import tpu as pltpu
from jax.sharding import PartitionSpec as P

MESH = pl.DeviceIdType.MESH
EXP = 4
CAP = 40
SIDE = 4
ROWS = SIDE * CAP
ALL_ROWS = SIDE * ROWS
HALF = ROWS // 2
ETS = 8
WIDE = 512
PART = 256
F32 = jnp.float32
BF16 = jnp.bfloat16
NT = (((1,), (1,)), ((), ()))
FLOWS = (0, 1)
VMEM_LIMIT = 62 * 1024 * 1024


def place():
    dp = lax.axis_index("dp")
    et = lax.axis_index("et")
    return lax.div(dp, SIDE), lax.rem(dp, SIDE), lax.div(et, 2), lax.rem(et, 2)


def turn(value, by):
    return lax.rem(value + by, SIDE)


def device(y, z, x, c):
    return (y * SIDE + z, x * 2 + c)


def remote(src, dst, send_sem, recv_sem, target):
    return pltpu.make_async_remote_copy(
        src_ref=src, dst_ref=dst, send_sem=send_sem, recv_sem=recv_sem, device_id=target, device_id_type=MESH
    )


def greet(y, z, x, c):
    barrier = pltpu.get_barrier_semaphore()
    others = [device(y, z, x, 1 - c)]
    others += [device(y, z, turn(x, 1), c), device(y, z, turn(x, 3), c)]
    others += [device(y, turn(z, 1), x, c), device(y, turn(z, 3), x, c)]
    others += [device(turn(y, by), z, x, c) for by in (1, 2, 3)]
    for other in others:
        pl.semaphore_signal(barrier, inc=1, device_id=other, device_id_type=MESH)
    return lambda: pl.semaphore_wait(barrier, len(others))


def halves_below(value):
    return jnp.concatenate([value[:, :PART], value[:, PART:]], axis=0)


def pack_rows(routes, probs, tok, cot, pack):
    count = tok.shape[0]
    slots = (CAP, count)
    route = routes[...].astype(F32)
    prob = probs[...]
    r0 = jnp.broadcast_to(route[0:1], slots)
    r1 = jnp.broadcast_to(route[1:2], slots)
    p0 = jnp.broadcast_to(prob[0:1], slots)
    p1 = jnp.broadcast_to(prob[1:2], slots)
    square = (count, count)
    first = lax.broadcasted_iota(jnp.int32, square, 0)
    second = lax.broadcasted_iota(jnp.int32, square, 1)
    before = jnp.where(first < second, 1.0, 0.0).astype(BF16)
    slot = lax.broadcasted_iota(jnp.int32, slots, 0).astype(F32)
    x_all = tok[...]
    d_all = cot[...]
    for e in range(EXP):
        in0 = jnp.where(r0 == e, 1.0, 0.0)
        in1 = jnp.where(r1 == e, 1.0, 0.0)
        member = in0 + in1
        placed = jnp.dot(member.astype(BF16), before, preferred_element_type=F32)
        pick = jnp.where(placed == slot, member, 0.0)
        weight = jnp.sum(pick * (in0 * p0 + in1 * p1), axis=1, keepdims=True)
        pick = pick.astype(BF16)
        chosen = jnp.dot(pick, x_all, preferred_element_type=F32)
        scaled = weight * jnp.dot(pick, d_all, preferred_element_type=F32)
        pack[0, e] = halves_below(chosen).astype(BF16)
        pack[1, e] = halves_below(scaled).astype(BF16)


def main_kernel(
    routes, probs, tok, cot, wg, wu, wd, gate_out, up_out, down_out, back_out,
    pack, recv, xb, sb, wgv, wuv, wdv, acc_g, acc_u, acc_d, hb, dgb, dub,
    own, psend, precv, far, farr, mid, midr, far2, far2r, mid2, mid2r, ysend, yrecv, ht, dt, stage_x, stage_s,
    w_sem, out_sem, ys, yr, n1r, h1r, n2r, h2r, ring_s, ps, pr, qs, qr, fr, mr, f2r, m2r, sum_s, bs, br,
):
    y, z, x, c = place()
    weights = ((wg, wgv), (wu, wuv), (wd, wdv))
    for i, (src, dst) in enumerate(weights):
        for k in range(ETS):
            pltpu.make_async_copy(src.at[:, pl.ds(k * WIDE, WIDE)], dst.at[k], w_sem.at[i]).start()

    def wait_bytes(ref, sem):
        pltpu.make_async_copy(ref, ref, sem).wait()

    await_greetings = greet(y, z, x, c)
    pack_rows(routes, probs, tok, cot, pack)
    await_greetings()

    for a in (0, 1):
        for by in (1, 2, 3):
            e = turn(y, by)
            remote(pack.at[a, e], recv.at[a, y], ys.at[a], yr.at[a], device(e, z, x, c)).start()

    bufs = (xb, sb)
    own_et = x * 2 + c
    partner = device(y, z, x, 1 - c)
    low, high = pl.ds(0, HALF), pl.ds(HALF, HALF)
    three = pl.ds(0, 3)

    def assemble(a):
        recv[a, y] = pack[a, y]
        wait_bytes(recv.at[a, three], yr.at[a])
        parts = [recv[a, i].astype(F32) for i in range(SIDE)]
        for h in FLOWS:
            piece = [part[h * CAP:(h + 1) * CAP] for part in parts]
            bufs[a][z, own_et * 2 + h] = jnp.concatenate(piece, axis=0).astype(BF16)

    def chunk(a, h, first, second):
        if h == 0:
            return bufs[a].at[second, (first * 2 + c) * 2]
        return bufs[a].at[first, (second * 2 + c) * 2 + 1]

    def mine(h):
        return (x, z) if h == 0 else (z, x)

    def on_x(by):
        return device(y, z, turn(x, by), c)

    def on_z(by):
        return device(y, turn(z, by), x, c)

    def first_dev(h, by):
        return on_x(by) if h == 0 else on_z(by)

    def second_dev(h, by):
        return on_z(by) if h == 0 else on_x(by)

    GO = (1, 3)
    COME = (3, 1)
    one_chunk = xb.at[0, 0]
    two_chunks = xb.at[0, pl.ds(0, 2)]

    def to_partner(a, h, i, j):
        f, s = mine(h)
        ref = chunk(a, h, turn(f, j), turn(s, i))
        remote(ref, ref, ps.at[a], pr.at[a, j if h == 0 else i], partner).start()

    def from_partner(a, group):
        wait_bytes(bufs[a].at[0, pl.ds(0, ETS)], pr.at[a, group])

    def first_send(a, h):
        f, s = mine(h)
        ref = chunk(a, h, f, s)
        for d in (0, 1):
            remote(ref, ref, ring_s.at[a], n1r.at[a, h], first_dev(h, GO[d])).start()

    def second_send(a, h, j):
        f, s = mine(h)
        ref = chunk(a, h, turn(f, j), s)
        for d in (0, 1):
            remote(ref, ref, ring_s.at[a], n2r.at[a, h, j], second_dev(h, GO[d])).start()
        to_partner(a, h, 0, j)

    def first_recv(a, h):
        f, s = mine(h)
        wait_bytes(two_chunks, n1r.at[a, h])
        for d in (0, 1):
            ref = chunk(a, h, turn(f, COME[d]), s).at[low if d == 0 else high]
            remote(ref, ref, ring_s.at[a], h1r.at[a, h], first_dev(h, GO[d])).start()
        second_send(a, h, 1)
        second_send(a, h, 3)

    def first_far(a, h):
        wait_bytes(one_chunk, h1r.at[a, h])
        second_send(a, h, 2)

    def second_recv(a, h, j):
        f, s = mine(h)
        wait_bytes(two_chunks, n2r.at[a, h, j])
        for d in (0, 1):
            ref = chunk(a, h, turn(f, j), turn(s, COME[d])).at[low if d == 0 else high]
            remote(ref, ref, ring_s.at[a], h2r.at[a, h, j], second_dev(h, GO[d])).start()
        for d in (0, 1):
            to_partner(a, h, COME[d], j)

    def second_far(a, h, j):
        wait_bytes(one_chunk, h2r.at[a, h, j])
        to_partner(a, h, 2, j)

    def rows_of(buf, k):
        left = buf[:, k * 2].reshape(ALL_ROWS, PART)
        right = buf[:, k * 2 + 1].reshape(ALL_ROWS, PART)
        return jnp.concatenate([left, right], axis=1)

    def gate_ready():
        wait_bytes(wgv, w_sem.at[0])
        wait_bytes(wuv, w_sem.at[1])
        wait_bytes(wdv, w_sem.at[2])

    def add_to(acc, value, first):
        if first:
            acc[...] = value
        else:
            acc[...] += value

    def gate_up(group, core):
        k = turn(x, group) * 2 + core
        first = group == 0 and core == 0
        rows = rows_of(xb, k)
        add_to(acc_g, lax.dot_general(rows, wgv[k], NT, preferred_element_type=F32), first)
        add_to(acc_u, lax.dot_general(rows, wuv[k], NT, preferred_element_type=F32), first)

    def d_hidden(group, core):
        k = turn(x, group) * 2 + core
        first = group == 0 and core == 0
        add_to(acc_d, lax.dot_general(rows_of(sb, k), wdv[k], NT, preferred_element_type=F32), first)

    STEPS = ALL_ROWS // 64

    def activate(part):
        def step(i, carry):
            rows = pl.ds(pl.multiple_of(i * 32, 32), 32)
            gate = acc_g[rows, :]
            up = acc_u[rows, :]
            squash = jax.nn.sigmoid(gate)
            active = gate * squash
            hb[rows, :] = (active * up).astype(BF16)
            acc_g[rows, :] = up * squash * (1.0 + gate * (1.0 - squash))
            acc_u[rows, :] = active
            return carry

        lax.fori_loop(part * STEPS, (part + 1) * STEPS, step, 0)

    def activate_back(part):
        def step(i, carry):
            rows = pl.ds(pl.multiple_of(i * 32, 32), 32)
            back = acc_d[rows, :]
            dgb[rows, :] = (back * acc_g[rows, :]).astype(BF16)
            dub[rows, :] = (back * acc_u[rows, :]).astype(BF16)
            return carry

        lax.fori_loop(part * STEPS, (part + 1) * STEPS, step, 0)

    stacked = (SIDE, ROWS, PART)

    def give_ready(b):
        if b == 1:
            wait_bytes(psend, qs)

    def pair_here(b, j):
        wait_bytes(precv.at[b, turn(x, j)], qr.at[b, j])

    def product(b, et):
        if b == 0:
            return jnp.dot(hb[...], wdv[et], preferred_element_type=F32)
        out = jnp.dot(dgb[...], wgv[et], preferred_element_type=F32)
        return out + jnp.dot(dub[...], wuv[et], preferred_element_type=F32)

    def give(b, j):
        at = turn(x, j)
        other = product(b, at * 2 + 1 - c).astype(BF16)
        psend[at, 0] = other[:, :PART].reshape(stacked)
        psend[at, 1] = other[:, PART:].reshape(stacked)
        remote(psend.at[at], precv.at[b, at], qs, qr.at[b, j], partner).start()

    def keep(b, j):
        at = turn(x, j)
        value = product(b, at * 2 + c)
        own[b, at, 0] = value[:, :PART].reshape(stacked)
        own[b, at, 1] = value[:, PART:].reshape(stacked)

    def ring1(h, by):
        return on_z(by) if h == 0 else on_x(by)

    def ring2(h, by):
        return on_x(by) if h == 0 else on_z(by)

    def spot(h, j, by):
        return (turn(x, j), turn(z, by)) if h == 0 else (turn(x, by), turn(z, j))

    def pair_sum(b, h, j, by):
        xx, zz = spot(h, j, by)
        return own[b, xx, h, zz] + precv[b, xx, h, zz].astype(F32)

    def send_far(b, h, j):
        far[b, h, j] = pair_sum(b, h, j, 2).astype(BF16)
        for d, part in ((0, high), (1, low)):
            remote(far.at[b, h, j, part], farr.at[b, h, j, d], sum_s.at[b], fr.at[b, h, j], ring1(h, GO[d])).start()

    def add_half(total, part, d):
        if d == 0:
            return jnp.concatenate([total[:HALF], total[HALF:] + part], axis=0)
        return jnp.concatenate([total[:HALF] + part, total[HALF:]], axis=0)

    def send_mid(b, h, j):
        wait_bytes(farr.at[b, h, j], fr.at[b, h, j])
        for d in (0, 1):
            total = add_half(pair_sum(b, h, j, GO[d]), farr[b, h, j, d].astype(F32), d)
            mid[b, h, j, d] = total.astype(BF16)
            remote(mid.at[b, h, j, d], midr.at[b, h, j, d], sum_s.at[b], mr.at[b, h, j], ring1(h, GO[d])).start()

    def finish_first(b, h, j):
        wait_bytes(midr.at[b, h, j], mr.at[b, h, j])
        xx, zz = spot(h, j, 0)
        total = pair_sum(b, h, j, 0)
        own[b, xx, h, zz] = total + midr[b, h, j, 0].astype(F32) + midr[b, h, j, 1].astype(F32)

    def first_sum(b, h, j):
        xx, zz = spot(h, j, 0)
        return own[b, xx, h, zz]

    def send_far2(b, h):
        far2[b, h] = first_sum(b, h, 2).astype(BF16)
        for d, part in ((0, high), (1, low)):
            remote(far2.at[b, h, part], far2r.at[b, h, d], sum_s.at[b], f2r.at[b, h], ring2(h, GO[d])).start()

    def send_mid2(b, h):
        wait_bytes(far2r.at[b, h], f2r.at[b, h])
        for d in (0, 1):
            total = add_half(first_sum(b, h, GO[d]), far2r[b, h, d].astype(F32), d)
            mid2[b, h, d] = total.astype(BF16)
            remote(mid2.at[b, h, d], mid2r.at[b, h, d], sum_s.at[b], m2r.at[b, h], ring2(h, GO[d])).start()

    def send_back(b):
        totals = []
        for h in FLOWS:
            wait_bytes(mid2r.at[b, h], m2r.at[b, h])
            total = first_sum(b, h, 0) + mid2r[b, h, 0].astype(F32) + mid2r[b, h, 1].astype(F32)
            totals.append(total)
        for i in range(SIDE):
            piece = [total[i * CAP:(i + 1) * CAP] for total in totals]
            ysend[b, i] = jnp.concatenate(piece, axis=0).astype(BF16)
        for by in (1, 2, 3):
            target = turn(y, by)
            remote(ysend.at[b, target], yrecv.at[b, y], bs.at[b], br.at[b], device(target, z, x, c)).start()
        yrecv[b, y] = ysend[b, y]

    def back_here(b):
        wait_bytes(yrecv.at[b, three], br.at[b])
        back_out[b] = yrecv[b]

    UNITS = wg.shape[0]

    def grads_ready():
        ht[...] = jnp.transpose(hb[...])
        dt[pl.ds(0, UNITS), :] = jnp.transpose(dgb[...])
        dt[pl.ds(UNITS, UNITS), :] = jnp.transpose(dub[...])

    def grad_copy(k, i):
        columns = pl.ds(k * WIDE, WIDE)
        slot = k % 2
        src = stage_s.at[slot] if i == 2 else stage_x.at[slot, pl.ds(i * UNITS, UNITS)]
        dst = (gate_out, up_out, down_out)[i]
        return pltpu.make_async_copy(src, dst.at[:, columns], out_sem.at[i, slot])

    def grad_x(k):
        if k > 1:
            grad_copy(k - 2, 0).wait()
            grad_copy(k - 2, 1).wait()
        stage_x[k % 2] = jnp.dot(dt[...], rows_of(xb, k), preferred_element_type=F32).astype(BF16)
        grad_copy(k, 0).start()
        grad_copy(k, 1).start()

    def grad_s(k):
        if k > 1:
            grad_copy(k - 2, 2).wait()
        stage_s[k % 2] = jnp.dot(ht[...], rows_of(sb, k), preferred_element_type=F32).astype(BF16)
        grad_copy(k, 2).start()

    assemble(0)
    first_send(0, 1)
    first_send(0, 0)
    second_send(0, 1, 0)
    second_send(0, 0, 0)
    first_recv(0, 1)
    gate_ready()
    first_recv(0, 0)
    second_recv(0, 0, 0)
    first_far(0, 1)
    second_recv(0, 1, 1)
    assemble(1)
    second_recv(0, 1, 0)
    second_recv(0, 0, 1)
    first_far(0, 0)
    second_recv(0, 0, 3)
    second_far(0, 0, 0)
    second_recv(0, 1, 3)
    first_send(1, 1)
    second_far(0, 0, 1)
    second_recv(0, 1, 2)
    first_send(1, 0)
    second_send(1, 1, 0)
    from_partner(0, 0)
    gate_up(0, 0)
    second_recv(0, 0, 2)
    second_send(1, 0, 0)
    gate_up(0, 1)
    second_far(0, 1, 0)
    second_far(0, 1, 3)
    second_far(0, 0, 3)
    from_partner(0, 1)
    second_far(0, 1, 1)
    gate_up(1, 0)
    second_far(0, 1, 2)
    first_recv(1, 1)
    first_recv(1, 0)
    second_far(0, 0, 2)
    gate_up(1, 1)
    from_partner(0, 3)
    gate_up(3, 0)
    second_recv(1, 0, 0)
    gate_up(3, 1)
    first_far(1, 1)
    second_recv(1, 1, 0)
    from_partner(0, 2)
    gate_up(2, 0)
    gate_up(2, 1)
    second_recv(1, 1, 1)
    second_recv(1, 0, 1)
    second_recv(1, 1, 3)
    activate(0)
    second_recv(1, 0, 3)
    first_far(1, 0)
    activate(1)
    give_ready(0)
    second_far(1, 0, 0)
    give(0, 2)
    keep(0, 2)
    give(0, 3)
    second_recv(1, 1, 2)
    second_far(1, 0, 1)
    keep(0, 3)
    give(0, 1)
    keep(0, 1)
    second_far(1, 0, 3)
    from_partner(1, 0)
    second_far(1, 1, 1)
    second_far(1, 1, 0)
    d_hidden(0, 0)
    give(0, 0)
    pair_here(0, 2)
    second_recv(1, 0, 2)
    send_far(0, 0, 2)
    send_far(0, 1, 2)
    second_far(1, 1, 3)
    send_far(0, 1, 1)
    d_hidden(0, 1)
    send_far(0, 1, 3)
    send_far(0, 1, 0)
    pair_here(0, 3)
    second_far(1, 1, 2)
    send_far(0, 0, 3)
    from_partner(1, 1)
    d_hidden(1, 0)
    d_hidden(1, 1)
    pair_here(0, 1)
    keep(0, 0)
    second_far(1, 0, 2)
    send_far(0, 0, 1)
    from_partner(1, 3)
    d_hidden(3, 0)
    d_hidden(3, 1)
    send_mid(0, 0, 2)
    send_mid(0, 1, 2)
    pair_here(0, 0)
    send_far(0, 0, 0)
    send_mid(0, 0, 3)
    send_mid(0, 1, 3)
    from_partner(1, 2)
    d_hidden(2, 0)
    d_hidden(2, 1)
    activate_back(0)
    activate_back(1)
    give_ready(1)
    give(1, 2)
    send_mid(0, 1, 0)
    keep(1, 2)
    give(1, 3)
    send_mid(0, 0, 1)
    keep(1, 3)
    give(1, 1)
    pair_here(1, 2)
    send_far(1, 1, 2)
    send_far(1, 0, 2)
    send_mid(0, 1, 1)
    send_mid(0, 0, 0)
    keep(1, 1)
    pair_here(1, 3)
    give(1, 0)
    send_far(1, 0, 3)
    send_far(1, 1, 3)
    keep(1, 0)
    send_mid(1, 0, 2)
    finish_first(0, 0, 2)
    send_far(1, 1, 1)
    pair_here(1, 1)
    send_far(1, 0, 1)
    send_mid(1, 1, 2)
    grads_ready()
    finish_first(0, 1, 3)
    pair_here(1, 0)
    finish_first(0, 1, 1)
    send_far2(0, 0)
    send_mid(1, 0, 3)
    send_mid(1, 1, 3)
    finish_first(0, 0, 0)
    send_far(1, 1, 0)
    finish_first(0, 1, 2)
    send_far(1, 0, 0)
    send_mid(1, 1, 1)
    send_far2(0, 1)
    finish_first(0, 1, 0)
    grad_x(0)
    finish_first(0, 0, 3)
    grad_s(0)
    finish_first(1, 1, 2)
    send_mid(1, 0, 1)
    finish_first(1, 0, 2)
    send_far2(1, 0)
    send_far2(1, 1)
    finish_first(0, 0, 1)
    grad_x(1)
    finish_first(1, 0, 3)
    grad_s(1)
    send_mid2(0, 0)
    send_mid2(0, 1)
    send_mid(1, 1, 0)
    grad_x(2)
    finish_first(1, 0, 1)
    send_mid(1, 0, 0)
    finish_first(1, 1, 3)
    finish_first(1, 1, 1)
    grad_s(2)
    send_mid2(1, 0)
    send_mid2(1, 1)
    grad_x(3)
    send_back(0)
    grad_s(3)
    grad_x(4)
    grad_s(4)
    finish_first(1, 0, 0)
    grad_x(5)
    finish_first(1, 1, 0)
    send_back(1)
    grad_s(5)
    grad_x(6)
    grad_s(6)
    grad_x(7)
    grad_s(7)
    back_here(0)
    back_here(1)

    for k in (ETS - 2, ETS - 1):
        for i in range(3):
            grad_copy(k, i).wait()
    wait_bytes(psend, qs)
    for a in (0, 1):
        wait_bytes(pack.at[a, three], ys.at[a])
        wait_bytes(ysend.at[a, three], bs.at[a])
        wait_bytes(bufs[a].at[:, pl.ds(0, ETS)], ps.at[a])
        thirty = bufs[a].at[pl.ds(0, 2), pl.ds(0, 15)]
        wait_bytes(thirty, ring_s.at[a])
        wait_bytes(thirty, sum_s.at[a])


def spread_back(routes, probs, back, layer_out, token_out):
    count = layer_out.shape[0]
    square = (count, count)
    route = routes[...].astype(F32)
    prob = probs[...]
    r0 = jnp.transpose(jnp.broadcast_to(route[0:1], square))
    r1 = jnp.transpose(jnp.broadcast_to(route[1:2], square))
    p0 = jnp.transpose(jnp.broadcast_to(prob[0:1], square))[:, 0:1]
    p1 = jnp.transpose(jnp.broadcast_to(prob[1:2], square))[:, 0:1]
    first = lax.broadcasted_iota(jnp.int32, square, 0)
    second = lax.broadcasted_iota(jnp.int32, square, 1)
    before = jnp.where(second < first, 1.0, 0.0).astype(BF16)
    lane = second.astype(F32)
    layer = [jnp.zeros((count, PART), F32) for _ in FLOWS]
    token = [jnp.zeros((count, PART), F32) for _ in FLOWS]
    for e in range(EXP):
        in0 = jnp.where(r0 == e, 1.0, 0.0)
        in1 = jnp.where(r1 == e, 1.0, 0.0)
        member = in0 + in1
        placed = jnp.dot(before, member.astype(BF16), preferred_element_type=F32)
        weight = in0[:, 0:1] * p0 + in1[:, 0:1] * p1
        for h in FLOWS:
            pick = jnp.where(placed + h * CAP == lane, member, 0.0)
            pick = jnp.where((lane >= h * CAP) & (lane < (h + 1) * CAP), pick, 0.0)
            pick = pick[:, :2 * CAP].astype(BF16)
            layer[h] = layer[h] + weight * jnp.dot(pick, back[0, e], preferred_element_type=F32)
            token[h] = token[h] + jnp.dot(pick, back[1, e], preferred_element_type=F32)
    layer_out[...] = jnp.concatenate(layer, axis=1).astype(BF16)
    token_out[...] = jnp.concatenate(token, axis=1).astype(BF16)


def finish_kernel(routes, probs, back, gate_in, up_in, down_in, layer_out, token_out, gate_out, up_out, down_out, held, sem):
    pairs = ((gate_in, gate_out), (up_in, up_out), (down_in, down_out))
    blocks = 4
    rows = gate_in.shape[0] // blocks

    def move(i, k, way):
        part = pl.ds(k * rows, rows)
        src, dst = pairs[i]
        if way == 0:
            return pltpu.make_async_copy(src.at[part], held.at[i, part], sem.at[0, i, k])
        return pltpu.make_async_copy(held.at[i, part], dst.at[part], sem.at[1, i, k])

    steps = [(i, k) for i in range(3) for k in range(blocks)]
    for i, k in steps:
        move(i, k, 0).start()
    for i, k in steps:
        move(i, k, 0).wait()
        move(i, k, 1).start()
    spread_back(routes, probs, back, layer_out, token_out)
    for i, k in steps:
        move(i, k, 1).wait()


def per_device(tokens, routes, route_probs, grad_out, w_gate, w_up, w_down):
    units, width = w_gate.shape
    count = tokens.shape[0]
    vmem = pl.BlockSpec(memory_space=pltpu.VMEM)
    anywhere = pl.BlockSpec(memory_space=pl.ANY)
    dma = pltpu.SemaphoreType.DMA
    back_shape = jax.ShapeDtypeStruct((2, EXP, 2 * CAP, PART), BF16)
    weight_buf = pltpu.VMEM((ETS, units, WIDE), BF16)
    gather_buf = pltpu.VMEM((SIDE, 2 * ETS, ROWS, PART), BF16)
    acc = pltpu.VMEM((ALL_ROWS, units), F32)
    hidden_buf = pltpu.VMEM((ALL_ROWS, units), BF16)
    packed = pltpu.VMEM((2, EXP, 2 * CAP, PART), BF16)
    routes_t = routes.T
    probs_t = route_probs.T
    grad_shape = jax.ShapeDtypeStruct((units, width), BF16)
    gate, up, down, back = pl.pallas_call(
        main_kernel,
        out_shape=(grad_shape, grad_shape, grad_shape, back_shape),
        in_specs=[vmem] * 4 + [anywhere] * 3,
        out_specs=(anywhere, anywhere, anywhere, vmem),
        scratch_shapes=[
            packed, packed, gather_buf, gather_buf, weight_buf, weight_buf, weight_buf,
            acc, acc, acc, hidden_buf, hidden_buf, hidden_buf,
            pltpu.VMEM((2, SIDE, 2, SIDE, ROWS, PART), F32),
            pltpu.VMEM((SIDE, 2, SIDE, ROWS, PART), BF16),
            pltpu.VMEM((2, SIDE, 2, SIDE, ROWS, PART), BF16),
            pltpu.VMEM((2, 2, SIDE, ROWS, PART), BF16),
            pltpu.VMEM((2, 2, SIDE, 2, HALF, PART), BF16),
            pltpu.VMEM((2, 2, SIDE, 2, ROWS, PART), BF16),
            pltpu.VMEM((2, 2, SIDE, 2, ROWS, PART), BF16),
            pltpu.VMEM((2, 2, ROWS, PART), BF16),
            pltpu.VMEM((2, 2, 2, HALF, PART), BF16),
            pltpu.VMEM((2, 2, 2, ROWS, PART), BF16),
            pltpu.VMEM((2, 2, 2, ROWS, PART), BF16),
            packed, packed,
            pltpu.VMEM((units, ALL_ROWS), BF16),
            pltpu.VMEM((2 * units, ALL_ROWS), BF16),
            pltpu.VMEM((2, 2 * units, WIDE), BF16),
            pltpu.VMEM((2, units, WIDE), BF16),
            dma((3,)), dma((3, 2)), dma((2,)), dma((2,)),
            dma((2, 2)), dma((2, 2)), dma((2, 2, 4)), dma((2, 2, 4)), dma((2,)), dma((2,)), dma((2, 4)),
            dma(()), dma((2, 4)), dma((2, 2, 4)), dma((2, 2, 4)), dma((2, 2)), dma((2, 2)), dma((2,)),
            dma((2,)), dma((2,)),
        ],
        compiler_params=pltpu.CompilerParams(collective_id=0, has_side_effects=True, vmem_limit_bytes=VMEM_LIMIT),
        name="expert_layer",
    )(routes_t, probs_t, tokens, grad_out, w_gate, w_up, w_down)

    token_shape = jax.ShapeDtypeStruct(tokens.shape, BF16)
    return pl.pallas_call(
        finish_kernel,
        out_shape=(token_shape, token_shape, grad_shape, grad_shape, grad_shape),
        in_specs=[vmem] * 3 + [anywhere] * 3,
        out_specs=(vmem, vmem, anywhere, anywhere, anywhere),
        scratch_shapes=[pltpu.VMEM((3, units, width), BF16), dma((2, 3, 4))],
        compiler_params=pltpu.CompilerParams(vmem_limit_bytes=VMEM_LIMIT),
        name="finish",
    )(routes_t, probs_t, back, gate, up, down)


def solution(mesh):
    return jax.shard_map(
        per_device,
        mesh=mesh,
        in_specs=(
            P("dp", "et"),
            P("dp", None),
            P("dp", None),
            P("dp", "et"),
            P(("dp", "et"), None),
            P(("dp", "et"), None),
            P(("dp", "et"), None),
        ),
        out_specs=(
            P("dp", "et"),
            P("dp", "et"),
            P(("dp", "et"), None),
            P(("dp", "et"), None),
            P(("dp", "et"), None),
        ),
        check_vma=False,
    )
```
